128 devices in a mesh: lat: 8 (over z, core), lon: 16 (over x, y).
Axes of the slice: x: 4, y: 4, z: 4, core: 2. Of those that a mesh axis runs over, the one named last changes fastest.
Arguments:
- obs_values: bfloat16 [128, 128, 64, 32], P(('lat', 'lon')), may hold values from -6 to 6
- kernel_weights: bfloat16 [128, 128, 64, 128], P(('lat', 'lon')), may hold values from 0.0099487305 to 1
- pixel_blocks: int32 [128, 128, 64], P(('lat', 'lon')), may hold values from 0 to 127
- obs_counts: int32 [128, 128], P(('lat', 'lon')), may hold values from 1 to 64, as said below
- kernel_one: float32 [3, 3, 64, 33], replicated, may hold values from -0.375 to 0.375
- kernel_two: float32 [3, 3, 64, 64], replicated, may hold values from -0.25 to 0.25
- cotangent: bfloat16 [64, 64, 2048], P(None, 'lat', 'lon'), may hold values from -0.015625 to 0.015625
Outputs:
- features: bfloat16 [64, 64, 2048], P(None, 'lat', 'lon')
- grad_kernel_one: float32 [3, 3, 64, 33], replicated
- grad_kernel_two: float32 [3, 3, 64, 64], replicated
The draws below stay inside these ranges and needn't reach their ends.
Inputs may be any that keep to these rules, and one draw needn't show every extreme that they name: `obs_counts`: every count is at least 1 and at most 64; in every draw some tile receives exactly 64 observations from every instrument shard, and the loads of tiles differ.
All inputs are finite; a program needn't handle non-finite values.
Results may differ from the reference program's by a relative error of at most 0.0014.
Values may be sent and summed in bfloat16 or wider, within the bound.
A program may use at most 64 MiB of HBM per device.

```python
import math
import jax
import jax.numpy as jnp
from jax import lax

C_OBS = 32
CH = 64
PIX = 128
H_DEV = 32
W_DEV = 512
CAP = 64
TILES = 128
C_IN = 33
BLOCKS = 128
ROWS_OUT = 64
COLS_OUT = 2048
N_LAT = 8
N_LON = 16


def draw_obs_counts(key, part):
    key_level = jax.random.fold_in(key, 11)
    key_pick = jax.random.fold_in(key, 12)
    key_base = jax.random.fold_in(key, 13)
    load_level = jax.random.randint(key_level, (TILES,), 1, 5)
    chosen = jax.random.randint(key_pick, (), 0, TILES)
    load_level = jnp.where(jnp.arange(TILES) == chosen, 4, load_level)
    base_count = jax.random.randint(key_base, (TILES, TILES), CAP // 2, CAP + 1)
    counts = jnp.minimum(CAP, base_count * load_level[None, :] // 2)
    return jnp.maximum(counts, 1).astype(jnp.int32)


def touch_ends(array, rng, low, top_value):
    extent = array.shape
    place = [jax.random.randint(jax.random.fold_in(rng, axis), (), 0, extent[axis]) for axis in range(len(extent))]
    array = array.at[tuple(place)].set(low)
    longest = extent.index(max(extent))
    place[longest] = (place[longest] + 1) % extent[longest]
    return array.at[tuple(place)].set(top_value)


def levels(stream_key, shape, split, smallest, largest):
    loudness, own = 1.0, jax.random.fold_in(stream_key, 6)
    for dim, parts in split:
        heights = jnp.exp(jax.random.uniform(jax.random.fold_in(own, dim), (parts,), jnp.float32, smallest / len(split), largest / len(split)))
        loudness = loudness * jnp.repeat(heights, shape[dim] // parts).reshape([-1 if axis == dim else 1 for axis in range(len(shape))])
    return loudness


def centred(stream_key, extent, spread, reach, split=(), kind=jnp.bfloat16):
    values = jax.random.normal(stream_key, extent, jnp.float32) * spread
    if len(split) > 0:
        values = levels(stream_key, extent, split, -0.22, 0.18) * values
    return jnp.clip(values, min=-reach, max=reach).astype(kind)


def setup_inputs(seed: int = 0) -> dict:
    key_list = jax.random.split(jax.random.key(seed), 8)
    return {
        "obs_values": centred(key_list[0], (TILES, TILES, CAP, C_OBS), 1.0, 6.0, ((0, 128),)),
        "kernel_weights": jnp.clip(jnp.exp(math.log(1.0) - 4.61031033 * jax.random.uniform(key_list[1], (TILES, TILES, CAP, PIX), jnp.float32) ** levels(key_list[1], (TILES, TILES, CAP, PIX), ((0, 128),), -0.2, 0.2)), 0.0099487305, 1.0).astype(jnp.bfloat16),
        "pixel_blocks": touch_ends(jax.random.randint(key_list[2], (TILES, TILES, CAP), 0, BLOCKS), jax.random.fold_in(key_list[2], 1), 0, BLOCKS - 1).astype(jnp.int32),
        "obs_counts": draw_obs_counts(jax.random.fold_in(key_list[7], 71), 0),
        "kernel_one": centred(key_list[4], (3, 3, CH, C_IN), (9 * C_IN) ** -0.5, 0.375, (), jnp.float32),
        "kernel_two": centred(key_list[5], (3, 3, CH, CH), (9 * CH) ** -0.5, 0.25, (), jnp.float32),
        "cotangent": centred(key_list[6], (CH, ROWS_OUT, COLS_OUT), 0.003, 0.015625, ((1, 8), (2, 16))),
    }


def stride_conv(padded, kernel, out_rows, out_cols):
    running = jnp.zeros((kernel.shape[2], out_rows, out_cols), padded.dtype)
    for row_off in range(3):
        for col_off in range(3):
            window = lax.slice(padded, (0, row_off, col_off), (padded.shape[0], row_off + 2 * out_rows - 1, col_off + 2 * out_cols - 1), (1, 2, 2))
            running = running + jnp.einsum('oc,chw->ohw', kernel[row_off, col_off], window, precision=lax.Precision.HIGHEST)
    return running

def global_rim(field):
    widened = jnp.concatenate([field[:, :, -1:], field], axis=2)
    return jnp.concatenate([jnp.zeros_like(widened[:, :1, :]), widened], axis=1)

def reference(obs_values, kernel_weights, pixel_blocks, obs_counts, kernel_one, kernel_two, cotangent):
    slot_index = jnp.arange(CAP, dtype=jnp.int32)

    def tile_grid(index):
        values_in = obs_values[:, index].astype(jnp.float32)
        weights_in = kernel_weights[:, index].astype(jnp.float32)
        blocks = pixel_blocks[:, index].reshape(-1)
        is_live = (slot_index[None, :] < obs_counts[:, index][:, None]).astype(jnp.float32)
        channels = jnp.concatenate([values_in * is_live[:, :, None], is_live[:, :, None]], axis=2)
        outer = channels[:, :, :, None] * weights_in[:, :, None, :]
        outer = outer.reshape(TILES * CAP, C_IN, PIX)
        summed = jax.ops.segment_sum(outer, blocks, num_segments=BLOCKS)
        summed = summed.reshape(H_DEV, W_DEV // PIX, C_IN, PIX).transpose(2, 0, 1, 3)
        return summed.reshape(C_IN, H_DEV, W_DEV)
    tiles = lax.map(tile_grid, jnp.arange(TILES, dtype=jnp.int32))
    grid_field = tiles.reshape(N_LAT, N_LON, C_IN, H_DEV, W_DEV).transpose(2, 0, 3, 1, 4)
    grid_field = grid_field.reshape(C_IN, N_LAT * H_DEV, N_LON * W_DEV)
    rows_one = N_LAT * H_DEV // 2
    cols_one = N_LON * W_DEV // 2

    def forward(first_kernel, second_kernel):
        pre_act = stride_conv(global_rim(grid_field), first_kernel, rows_one, cols_one)
        activation = jax.nn.silu(pre_act)
        return stride_conv(global_rim(activation), second_kernel, rows_one // 2, cols_one // 2)
    result, pull_back = jax.vjp(forward, kernel_one, kernel_two)
    grad_one, grad_two = pull_back(cotangent.astype(result.dtype))
    return (result.astype(jnp.bfloat16), grad_one, grad_two)
```

```python
import functools
import jax
import jax.numpy as jnp
from jax import lax
from jax.experimental import pallas as pl
from jax.experimental.pallas import tpu as pltpu
from jax.sharding import PartitionSpec as P

MESH = pl.DeviceIdType.MESH
F32, BF16 = jnp.float32, jnp.bfloat16
N = 128
CAP = 64
GROUP = 16
STEPS = N // GROUP
SLOTS = GROUP * CAP
ROWS = 32
C_OBS = 32


def position():
    return lax.axis_index("lat"), lax.axis_index("lon")


def partner(lat, lon, ordinal, sign):
    mixed = lax.rem(ordinal * 37, N)
    core = lax.rem(mixed, 2)
    dz = lax.rem(mixed // 2, 4)
    dx = lax.rem(mixed // 8, 4)
    dy = mixed // 32
    z = lax.rem(lat // 2 + sign * dz + 4, 4)
    c = lax.rem(lat + core, 2)
    x = lax.rem(lon // 4 + sign * dx + 4, 4)
    y = lax.rem(lon + sign * dy + 4, 4)
    return z * 2 + c, x * 4 + y


def greet_all(lat, lon):
    barrier = pltpu.get_barrier_semaphore()

    def greet(step, carry):
        to_lat = lax.rem(lat + step, 8)
        for d in range(16):
            @pl.when(jnp.logical_or(step > 0, d > 0))
            def _():
                pl.semaphore_signal(
                    barrier, inc=1, device_id=(to_lat, lax.rem(lon + d, 16)), device_id_type=MESH
                )
        return carry

    lax.fori_loop(0, 8, greet, 0)
    return barrier


def pack_values(values_ref, wide_ref, turned_ref, packed_ref):
    wide_ref[...] = values_ref[...].astype(F32)
    for i in range(16):
        pair = jnp.concatenate([wide_ref[:, i, :], wide_ref[:, 16 + i, :]], axis=0)
        turned_ref[:, i, :] = pair.T
    packed_ref[...] = turned_ref[...].astype(BF16)


def pack_codes(blocks_ref, counts_ref, codes_ref):
    slot = lax.broadcasted_iota(jnp.int32, (CAP, N), 0)
    code = jnp.where(slot < counts_ref[...], blocks_ref[...], 4 * ROWS)
    turned = jnp.concatenate([code, code], axis=0).astype(F32).T.astype(jnp.int32)
    codes_ref[:, 0, :] = turned


def spread_group(step, got_w, got_v, got_c, perm_ref, lhs_ref, rhs_ref, acc_ref):
    first = step * GROUP
    lane = lax.broadcasted_iota(jnp.int32, (1, N), 1)
    codes = got_c[pl.ds(first, GROUP), 0, :]
    row_parts, value_parts = [], []
    for p in range(GROUP // 2):
        even, odd = codes[2 * p : 2 * p + 1], codes[2 * p + 1 : 2 * p + 2]
        row_parts.append(jnp.where(lane < CAP, even, odd))
        one = got_v[first + 2 * p].astype(F32)
        two = got_v[first + 2 * p + 1].astype(F32)
        upper = jnp.where(lane < CAP, one, pltpu.roll(two, CAP, 1))
        lower = jnp.where(lane < CAP, pltpu.roll(one, CAP, 1), two)
        value_parts.append(jnp.concatenate([upper, lower], axis=0))
    row_of = jnp.broadcast_to(jnp.concatenate(row_parts, axis=1) // 4, (C_OBS, SLOTS)).astype(F32).astype(BF16)
    values = jnp.concatenate(value_parts, axis=1).astype(BF16)
    zero = jnp.zeros_like(values)
    for r in range(ROWS):
        lhs_ref[r * C_OBS : (r + 1) * C_OBS, :] = jnp.where(row_of == jnp.array(r, BF16), values, zero)
    rows = lax.broadcasted_iota(jnp.int32, (ROWS, SLOTS), 0).astype(F32).astype(BF16)
    lhs_ref[ROWS * C_OBS :, :] = jnp.where(row_of == rows, jnp.ones_like(values), zero)
    quarter = lax.rem(codes, 4).astype(F32).T
    lane_quarter = (lax.broadcasted_iota(jnp.int32, (CAP, N), 1) // 32).astype(F32)
    for s in range(GROUP):
        keep = jnp.where(quarter[:CAP, s : s + 1] == lane_quarter, 1.0, 0.0).astype(BF16)
        pixels = jnp.dot(got_w[first + s], perm_ref[...], preferred_element_type=F32).astype(BF16)
        for phase in range(4):
            rhs_ref[s * CAP : (s + 1) * CAP, phase * N : (phase + 1) * N] = (
                pixels[:, phase * N : (phase + 1) * N] * keep
            )
    acc_ref[...] += jnp.dot(lhs_ref[...], rhs_ref[...], preferred_element_type=F32)


def exchange_kernel(
    values_ref, w_ref, blocks_ref, counts_ref, perm_ref, acc_ref,
    wide, turned, packed, codes, got_w, got_v, got_c, lhs, rhs,
    sent, came_w, came_v, came_c, own,
):
    lat, lon = position()
    me = lat * 16 + lon
    barrier = greet_all(lat, lon)
    pack_values(values_ref, wide, turned, packed)
    pack_codes(blocks_ref, counts_ref, codes)
    acc_ref[...] = jnp.zeros_like(acc_ref)
    mine = [
        pltpu.make_async_copy(w_ref.at[me], got_w.at[0], own.at[0]),
        pltpu.make_async_copy(packed.at[me], got_v.at[0], own.at[1]),
        pltpu.make_async_copy(codes.at[me], got_c.at[0], own.at[2]),
    ]
    for copy in mine:
        copy.start()
    pl.semaphore_wait(barrier, N - 1)

    def send(ordinal, carry):
        to_lat, to_lon = partner(lat, lon, ordinal, 1)
        to = to_lat * 16 + to_lon
        step = ordinal // GROUP
        for k, (source, target, came) in enumerate(
            ((w_ref, got_w, came_w), (packed, got_v, came_v), (codes, got_c, came_c))
        ):
            pltpu.make_async_remote_copy(
                src_ref=source.at[to], dst_ref=target.at[ordinal], send_sem=sent.at[k],
                recv_sem=came.at[step], device_id=(to_lat, to_lon), device_id_type=MESH,
            ).start()
        return carry

    lax.fori_loop(1, N, send, 0)
    for copy in mine:
        copy.wait()

    def arrive(first, count, step):
        for source, target, came in ((w_ref, got_w, came_w), (packed, got_v, came_v), (codes, got_c, came_c)):
            pltpu.make_async_copy(
                target.at[pl.ds(first, count)], target.at[pl.ds(first, count)], came.at[step]
            ).wait()

    def work(step, carry):
        @pl.when(step == 0)
        def _():
            arrive(1, GROUP - 1, 0)

        @pl.when(step > 0)
        def _():
            arrive(step * GROUP, GROUP, step)

        spread_group(step, got_w, got_v, got_c, perm_ref, lhs, rhs, acc_ref)
        return carry

    lax.fori_loop(0, STEPS, work, 0)
    for k, source in enumerate((got_w, got_v, got_c)):
        pltpu.make_async_copy(source.at[pl.ds(0, N - 1)], source.at[pl.ds(0, N - 1)], sent.at[k]).wait()


def phase_picker():
    lane = jnp.arange(4 * N, dtype=jnp.int32)
    source = 4 * (lane % 32) + lane // N
    return (jnp.arange(N, dtype=jnp.int32)[:, None] == source[None, :]).astype(BF16)


def exchange(values, weights, blocks, counts):
    return pl.pallas_call(
        exchange_kernel,
        out_shape=jax.ShapeDtypeStruct((ROWS * C_OBS + ROWS, 4 * N), F32),
        in_specs=[
            pl.BlockSpec(memory_space=pltpu.VMEM),
            pl.BlockSpec(memory_space=pl.ANY),
            pl.BlockSpec(memory_space=pltpu.VMEM),
            pl.BlockSpec(memory_space=pltpu.VMEM),
            pl.BlockSpec(memory_space=pltpu.VMEM),
        ],
        out_specs=pl.BlockSpec(memory_space=pltpu.VMEM),
        scratch_shapes=[
            pltpu.VMEM((CAP, C_OBS, N), F32),
            pltpu.VMEM((N, 16, N), F32),
            pltpu.VMEM((N, 16, N), BF16),
            pltpu.VMEM((N, 1, N), jnp.int32),
            pltpu.VMEM((N, CAP, N), BF16),
            pltpu.VMEM((N, 16, N), BF16),
            pltpu.VMEM((N, 1, N), jnp.int32),
            pltpu.VMEM((ROWS * C_OBS + ROWS, SLOTS), BF16),
            pltpu.VMEM((SLOTS, 4 * N), BF16),
            pltpu.SemaphoreType.DMA((3,)),
            pltpu.SemaphoreType.DMA((STEPS,)),
            pltpu.SemaphoreType.DMA((STEPS,)),
            pltpu.SemaphoreType.DMA((STEPS,)),
            pltpu.SemaphoreType.DMA((3,)),
        ],
        compiler_params=pltpu.CompilerParams(collective_id=0, has_side_effects=True, vmem_limit_bytes=48 << 20),
    )(
        values.transpose(1, 2, 0), weights, blocks.T, counts[None, :], phase_picker()
    )


def send_to(source, target, sent, came, device):
    return pltpu.make_async_remote_copy(
        src_ref=source, dst_ref=target, send_sem=sent, recv_sem=came, device_id=device, device_id_type=MESH
    )


def all_sum(lat, lon, part_ref, total_ref, by_lat, by_y, by_x, sent, came):
    x, y = lon // 4, lax.rem(lon, 4)
    rows = lambda at: pl.ds(pl.multiple_of(8 * at, 8), 8)
    copies = []
    for d in range(1, 8):
        to = lax.rem(lat + d, 8)
        copies.append(send_to(part_ref.at[rows(to)], by_lat.at[d], sent.at[d], came.at[d], (to, lon)))
    for copy in copies:
        copy.start()
    for copy in copies:
        copy.wait()
    total = part_ref[rows(lat), :]
    for d in range(1, 8):
        total = total + by_lat[d]
    for base, slots, here in ((8, by_y, y), (12, by_x, x)):
        slots[here] = total
        copies = []
        for d in range(1, 4):
            to_lon = x * 4 + lax.rem(y + d, 4) if base == 8 else lax.rem(x + d, 4) * 4 + y
            copies.append(send_to(slots.at[here], slots.at[here], sent.at[base + d], came.at[base + d], (lat, to_lon)))
        for copy in copies:
            copy.start()
        for copy in copies:
            copy.wait()
        total = (slots[0] + slots[1]) + (slots[2] + slots[3])
    total_ref[rows(lat), :] = total
    copies = []
    for d in range(1, 8):
        to = lax.rem(lat + d, 8)
        copies.append(send_to(total_ref.at[rows(lat)], total_ref.at[rows(lat)], sent.at[16 + d], came.at[16 + d], (to, lon)))
    for copy in copies:
        copy.start()
    for copy in copies:
        copy.wait()


def sum_kernel(part_ref, total_ref, by_lat, by_y, by_x, sent, came):
    lat, lon = position()
    x, y = lon // 4, lax.rem(lon, 4)
    barrier = pltpu.get_barrier_semaphore()
    for d in range(1, 8):
        pl.semaphore_signal(barrier, inc=1, device_id=(lax.rem(lat + d, 8), lon), device_id_type=MESH)
    for d in range(1, 4):
        pl.semaphore_signal(barrier, inc=1, device_id=(lat, x * 4 + lax.rem(y + d, 4)), device_id_type=MESH)
        pl.semaphore_signal(barrier, inc=1, device_id=(lat, lax.rem(x + d, 4) * 4 + y), device_id_type=MESH)
    pl.semaphore_wait(barrier, 13)
    all_sum(lat, lon, part_ref, total_ref, by_lat, by_y, by_x, sent, came)


def summed_over_devices(part):
    width = part.shape[1]
    return pl.pallas_call(
        sum_kernel,
        out_shape=jax.ShapeDtypeStruct(part.shape, F32),
        in_specs=[pl.BlockSpec(memory_space=pltpu.VMEM)],
        out_specs=pl.BlockSpec(memory_space=pltpu.VMEM),
        scratch_shapes=[
            pltpu.VMEM((8, 8, width), F32),
            pltpu.VMEM((4, 8, width), F32),
            pltpu.VMEM((4, 8, width), F32),
            pltpu.SemaphoreType.DMA((24,)),
            pltpu.SemaphoreType.DMA((24,)),
        ],
        compiler_params=pltpu.CompilerParams(collective_id=1, has_side_effects=True),
    )(part)


H_DEV = 32
W_DEV = 512


def passed_along(block, axis, distance):
    devices = range(lax.axis_size(axis))
    route = [((i - distance) % len(devices), i) for i in devices]
    return lax.ppermute(block, axis, route)


def shifted_2(value, axis, steps):
    count = lax.axis_size(axis)
    leading, last = (max(0, -steps), min(count, count - steps))
    return lax.ppermute(value, axis, [(source, source + steps) for source in range(leading, last)])


def silu_slope(values_in):
    sigmoid_val = jax.nn.sigmoid(values_in)
    return sigmoid_val * (1.0 + values_in * (1.0 - sigmoid_val))


def column_phases(field):
    chans, rows, cols = field.shape
    half = cols // 2
    target = jnp.arange(cols, dtype=jnp.int32)
    source = jnp.where(target < half, 2 * target, 2 * (target - half) + 1)
    picker = (jnp.arange(cols, dtype=jnp.int32)[:, None] == source[None, :]).astype(jnp.float32)
    moved = jnp.dot(field.reshape(chans * rows, cols), picker, precision=lax.Precision.HIGHEST)
    moved = moved.reshape(chans, rows, cols)
    return (moved[:, :, :half], moved[:, :, half:])


def column_inputs(field, west_col):
    even_cols, odd_cols = column_phases(field)
    shifted = jnp.concatenate([west_col, odd_cols[:, :, :-1]], axis=2)
    return jnp.stack([shifted, even_cols, odd_cols])


def conv_taps(col_stack, north_rows, kernel):
    taps, chans, rows, half = col_stack.shape
    split_rows = col_stack.reshape(taps, chans, rows // 2, 2, half)
    even_rows = split_rows[:, :, :, 0, :]
    odd_rows = split_rows[:, :, :, 1, :]
    shifted = jnp.concatenate([north_rows, odd_rows[:, :, :-1, :]], axis=2)
    pieces = jnp.stack([shifted, even_rows, odd_rows])
    return jnp.einsum("aeoc,aechw->ohw", kernel, pieces, precision=lax.Precision.HIGHEST)


def layer_inputs(field):
    west_col = passed_along(field[:, :, -1:], "lon", 1)
    col_stack = column_inputs(field, west_col)
    north_rows = shifted_2(col_stack[:, :, -1:, :], "lat", 1)
    return (west_col, col_stack, north_rows)


def on_device(
    obs_values, kernel_weights, pixel_blocks, obs_counts, kernel_one, kernel_two, cotangent
):
    summed = exchange(obs_values[0], kernel_weights[0], pixel_blocks[0], obs_counts[0])
    main = summed[: ROWS * C_OBS].reshape(ROWS, C_OBS, 4, N).transpose(1, 0, 3, 2)
    density = summed[ROWS * C_OBS :].reshape(1, ROWS, 4, N).transpose(0, 1, 3, 2)
    grid_field = jnp.concatenate([main, density]).reshape(C_OBS + 1, H_DEV, W_DEV)
    grad_out = cotangent.astype(jnp.float32)
    west_one, stack_one, north_one = layer_inputs(grid_field)

    def first_layer(kernel):
        return conv_taps(stack_one, north_one, kernel)

    pre_act, pull_one = jax.vjp(first_layer, kernel_one)
    activation = jax.nn.silu(pre_act)
    west_two, stack_two, north_two = layer_inputs(activation)
    result, pull_two = jax.vjp(conv_taps, stack_two, north_two, kernel_two)
    grad_stack, grad_north, grad_two = pull_two(grad_out)
    grad_south = shifted_2(grad_north.astype(jnp.bfloat16), "lat", -1).astype(grad_north.dtype)
    grad_stack = jnp.concatenate(
        [grad_stack[:, :, :-1, :], grad_stack[:, :, -1:, :] + grad_south], axis=2
    )
    _, pull_cols = jax.vjp(column_inputs, activation, west_two)
    grad_act, grad_west = pull_cols(grad_stack)
    grad_east = passed_along(grad_west, "lon", -1)
    grad_act = jnp.concatenate([grad_act[:, :, :-1], grad_act[:, :, -1:] + grad_east], axis=2)
    grad_pre = grad_act * silu_slope(pre_act)
    grad_one = pull_one(grad_pre)[0]
    flat = jnp.concatenate([grad_one.reshape(-1), grad_two.reshape(-1)])
    flat = jnp.pad(flat, (0, 64 * 896 - flat.shape[0])).reshape(64, 896)
    flat = summed_over_devices(flat).reshape(-1)
    grad_one, grad_two = (
        flat[: grad_one.size].reshape(grad_one.shape),
        flat[grad_one.size : grad_one.size + grad_two.size].reshape(grad_two.shape),
    )
    return (result.astype(jnp.bfloat16), grad_one, grad_two)


def solution(mesh):
    placed = (
        P(("lat", "lon"), None, None, None),
        P(("lat", "lon"), None, None, None),
        P(("lat", "lon"), None, None),
        P(("lat", "lon"), None),
        P(),
        P(),
        P(None, "lat", "lon"),
    )
    return jax.shard_map(
        on_device,
        mesh=mesh,
        in_specs=placed,
        out_specs=(P(None, "lat", "lon"), P(), P()),
        check_vma=False,
    )
```

```python
import jax
import jax.numpy as jnp
from jax import lax
from jax.experimental import pallas as pl
from jax.experimental.pallas import tpu as pltpu
from jax.sharding import PartitionSpec as P

MESH = pl.DeviceIdType.MESH
F32, BF16 = jnp.float32, jnp.bfloat16
N = 128
CAP = 64
GROUP = 16
STEPS = N // GROUP
SLOTS = GROUP * CAP
ROWS = 32
C_OBS = 32


def position():
    return lax.axis_index("lat"), lax.axis_index("lon")


def partner(lat, lon, ordinal, sign):
    mixed = lax.rem(ordinal * 37, N)
    core = lax.rem(mixed, 2)
    dz = lax.rem(mixed // 2, 4)
    dx = lax.rem(mixed // 8, 4)
    dy = mixed // 32
    z = lax.rem(lat // 2 + sign * dz + 4, 4)
    c = lax.rem(lat + core, 2)
    x = lax.rem(lon // 4 + sign * dx + 4, 4)
    y = lax.rem(lon + sign * dy + 4, 4)
    return z * 2 + c, x * 4 + y


def greet_all(lat, lon):
    barrier = pltpu.get_barrier_semaphore()

    def greet(step, carry):
        to_lat = lax.rem(lat + step, 8)
        for d in range(16):
            @pl.when(jnp.logical_or(step > 0, d > 0))
            def _():
                pl.semaphore_signal(
                    barrier, inc=1, device_id=(to_lat, lax.rem(lon + d, 16)), device_id_type=MESH
                )
        return carry

    lax.fori_loop(0, 8, greet, 0)
    return barrier


def pack_values(values_ref, wide_ref, turned_ref, packed_ref):
    wide_ref[...] = values_ref[...].astype(F32)
    for i in range(16):
        pair = jnp.concatenate([wide_ref[:, i, :], wide_ref[:, 16 + i, :]], axis=0)
        turned_ref[:, i, :] = pair.T
    packed_ref[...] = turned_ref[...].astype(BF16)


def pack_codes(blocks_ref, counts_ref, codes_ref):
    slot = lax.broadcasted_iota(jnp.int32, (CAP, N), 0)
    code = jnp.where(slot < counts_ref[...], blocks_ref[...], 4 * ROWS)
    turned = jnp.concatenate([code, code], axis=0).astype(F32).T.astype(jnp.int32)
    codes_ref[:, 0, :] = turned


def spread_group(step, got_w, got_v, got_c, perm_ref, lhs_ref, rhs_ref, acc_ref):
    first = step * GROUP
    lane = lax.broadcasted_iota(jnp.int32, (1, N), 1)
    codes = got_c[pl.ds(first, GROUP), 0, :]
    row_parts, value_parts = [], []
    for p in range(GROUP // 2):
        even, odd = codes[2 * p : 2 * p + 1], codes[2 * p + 1 : 2 * p + 2]
        row_parts.append(jnp.where(lane < CAP, even, odd))
        one = got_v[first + 2 * p].astype(F32)
        two = got_v[first + 2 * p + 1].astype(F32)
        upper = jnp.where(lane < CAP, one, pltpu.roll(two, CAP, 1))
        lower = jnp.where(lane < CAP, pltpu.roll(one, CAP, 1), two)
        value_parts.append(jnp.concatenate([upper, lower], axis=0))
    row_of = jnp.broadcast_to(jnp.concatenate(row_parts, axis=1) // 4, (C_OBS, SLOTS)).astype(F32).astype(BF16)
    values = jnp.concatenate(value_parts, axis=1).astype(BF16)
    zero = jnp.zeros_like(values)
    for r in range(ROWS):
        lhs_ref[r * C_OBS : (r + 1) * C_OBS, :] = jnp.where(row_of == jnp.array(r, BF16), values, zero)
    rows = lax.broadcasted_iota(jnp.int32, (ROWS, SLOTS), 0).astype(F32).astype(BF16)
    lhs_ref[ROWS * C_OBS :, :] = jnp.where(row_of == rows, jnp.ones_like(values), zero)
    quarter = lax.rem(codes, 4).astype(F32).T
    lane_quarter = (lax.broadcasted_iota(jnp.int32, (CAP, N), 1) // 32).astype(F32)
    for s in range(GROUP):
        keep = jnp.where(quarter[:CAP, s : s + 1] == lane_quarter, 1.0, 0.0).astype(BF16)
        pixels = jnp.dot(got_w[first + s], perm_ref[...], preferred_element_type=F32).astype(BF16)
        for phase in range(4):
            rhs_ref[s * CAP : (s + 1) * CAP, phase * N : (phase + 1) * N] = (
                pixels[:, phase * N : (phase + 1) * N] * keep
            )
    acc_ref[...] += jnp.dot(lhs_ref[...], rhs_ref[...], preferred_element_type=F32)


def send_to(source, target, sent, came, device):
    return pltpu.make_async_remote_copy(
        src_ref=source, dst_ref=target, send_sem=sent, recv_sem=came, device_id=device, device_id_type=MESH
    )


def all_sum(lat, lon, part_ref, total_ref, by_lat, by_y, by_x, sent, came):
    x, y = lon // 4, lax.rem(lon, 4)
    rows = lambda at: pl.ds(pl.multiple_of(8 * at, 8), 8)
    copies = []
    for d in range(1, 8):
        to = lax.rem(lat + d, 8)
        copies.append(send_to(part_ref.at[rows(to)], by_lat.at[d], sent.at[d], came.at[d], (to, lon)))
    for copy in copies:
        copy.start()
    for copy in copies:
        copy.wait()
    total = part_ref[rows(lat), :]
    for d in range(1, 8):
        total = total + by_lat[d]
    for base, slots, here in ((8, by_y, y), (12, by_x, x)):
        slots[here] = total
        copies = []
        for d in range(1, 4):
            to_lon = x * 4 + lax.rem(y + d, 4) if base == 8 else lax.rem(x + d, 4) * 4 + y
            copies.append(send_to(slots.at[here], slots.at[here], sent.at[base + d], came.at[base + d], (lat, to_lon)))
        for copy in copies:
            copy.start()
        for copy in copies:
            copy.wait()
        total = (slots[0] + slots[1]) + (slots[2] + slots[3])
    total_ref[rows(lat), :] = total
    copies = []
    for d in range(1, 8):
        to = lax.rem(lat + d, 8)
        copies.append(send_to(total_ref.at[rows(lat)], total_ref.at[rows(lat)], sent.at[16 + d], came.at[16 + d], (to, lon)))
    for copy in copies:
        copy.start()
    for copy in copies:
        copy.wait()

CH = 64
STEP_ONE = 5 * C_OBS
STEP_TWO = 3 * CH


def halves(value):
    high = value.astype(BF16)
    return high, (value - high.astype(F32)).astype(BF16)


def dot_nt(a, b):
    return lax.dot_general(a, b, (((1,), (1,)), ((), ())), preferred_element_type=F32)


def dot(a, b):
    return jnp.dot(a, b, preferred_element_type=F32)


def lanes(rows):
    return lax.broadcasted_iota(jnp.int32, (rows, N), 1)


def pack_column(total, place, column):
    return jnp.where(lanes(total.shape[0]) == place, jnp.broadcast_to(column, total.shape), total)


def enter_west(value, column):
    moved = pltpu.roll(value, 1, 1)
    return jnp.where(lanes(value.shape[0]) == 0, jnp.broadcast_to(column, value.shape), moved)


def enter_east(value, column):
    moved = pltpu.roll(value, N - 1, 1)
    return jnp.where(lanes(value.shape[0]) == N - 1, jnp.broadcast_to(column, value.shape), moved)


def arrange_kernels(one_ref, two_ref, wide_one, wide_adj, wide_two, left_one, left_adj, left_two):
    wide_one[...] = jnp.zeros_like(wide_one)
    wide_adj[...] = jnp.zeros_like(wide_adj)
    for a in range(3):
        for tap in range(5):
            row = a * STEP_ONE + tap * C_OBS
            thin = 3 * STEP_ONE + a * 8 + tap
            for half, e in ((0, tap), (1, tap - 2)):
                if 0 <= e < 3:
                    at = slice(half * CH, half * CH + CH)
                    wide_one[row : row + C_OBS, at] = one_ref[a, e, :C_OBS, :]
                    wide_one[thin : thin + 1, at] = one_ref[a, e, C_OBS:, :]
        for e in range(3):
            at = (a * 3 + e) * CH
            wide_two[:, at : at + CH] = two_ref[a, e]
    for lower in range(2):
        for east in range(2):
            for down in range(lower + 1):
                for right in range(east + 1):
                    a = 1 if lower == 0 else 2 - 2 * down
                    e = 1 if east == 0 else 2 - 2 * right
                    row, col = (down * 2 + right) * CH, (lower * 2 + east) * CH
                    wide_adj[row : row + CH, col : col + CH] = two_ref[a, e]
    for wide, left, turn in ((wide_one, left_one, True), (wide_adj, left_adj, True), (wide_two, left_two, False)):
        value = wide[...].T if turn else wide[...]
        high, low = halves(value)
        rows = value.shape[0]
        left[:rows, :] = high
        left[rows:, :] = low


def arrange_cotangent(cot_ref, wide_cot, cot, cot_col):
    wide_cot[...] = cot_ref[...].astype(F32)
    packed = jnp.zeros((CH, N), F32)
    for g in range(8):
        value = wide_cot[:, g, :]
        cot[g] = value
        packed = pack_column(packed, g, value[:, :1])
    cot_col[...] = packed


def back_to_activation(lat, cot, from_south, from_east, from_corner, right, left_adj, grad_act):
    cot[8] = jnp.where(lat < 7, from_south[...], 0.0)
    edge = from_east[...]
    for g in range(9):
        column = edge[:, g : g + 1] if g < 8 else jnp.where(lat < 7, from_corner[:, :1], 0.0)
        right[g] = enter_east(cot[g], column)

    def pair(p, carry):
        stack = [
            jnp.concatenate([cot[g], right[g], cot[g + 1], right[g + 1]], axis=0).astype(BF16)
            for g in (2 * p, 2 * p + 1)
        ]
        both = dot(left_adj[...], jnp.concatenate(stack, axis=1))
        both = both[:256] + both[256:]
        grad_act[2 * p] = both[:, :N]
        grad_act[2 * p + 1] = both[:, N:]
        return carry

    lax.fori_loop(0, 4, pair, 0)


def split_row(r, rows_of, edge, high_ref, low_ref):
    phases = [rows_of(phase) for phase in range(4)]
    taps = [enter_west(phases[3], edge)] + phases
    high, low = halves(jnp.concatenate(taps, axis=0))
    high_ref[r] = high
    low_ref[r] = low


def field_edges(acc_ref, edge_ref):
    packed = jnp.zeros((C_OBS, N), F32)
    for r in range(ROWS):
        packed = pack_column(packed, r, acc_ref[r * C_OBS : (r + 1) * C_OBS, 4 * N - 1 :])
    edge_ref[:C_OBS, :] = packed
    edge_ref[C_OBS:, :] = acc_ref[ROWS * C_OBS :, 3 * N :]


def split_field(lat, acc_ref, north, north_thin, from_west, from_corner, thin, high_ref, low_ref, thin_high, thin_low):
    for r in range(ROWS):
        split_row(
            r + 1,
            lambda phase, r=r: acc_ref[r * C_OBS : (r + 1) * C_OBS, phase * N : (phase + 1) * N],
            from_west[:C_OBS, r : r + 1], high_ref, low_ref,
        )
    inside = lat > 0
    split_row(
        0,
        lambda phase: jnp.where(inside, north[:, phase * N : (phase + 1) * N], 0.0),
        jnp.where(inside, from_corner[:C_OBS, ROWS - 1 : ROWS], 0.0), high_ref, low_ref,
    )
    thin[...] = jnp.zeros_like(thin)
    for phase in range(4):
        at = slice(phase * N, (phase + 1) * N)
        thin[1 : ROWS + 1, phase + 1, :] = acc_ref[ROWS * C_OBS :, at]
        thin[0, phase + 1 : phase + 2, :] = jnp.where(inside, north_thin[7:8, at], 0.0)
    thin[1 : ROWS + 1, 0, :] = enter_west(acc_ref[ROWS * C_OBS :, 3 * N :], from_west[C_OBS:, N - 1 :])
    corner = enter_west(north_thin[7:8, 3 * N :], from_corner[2 * C_OBS - 1 :, N - 1 :])
    thin[0, 0:1, :] = jnp.where(inside, corner, 0.0)
    for h in range(ROWS // 2):
        rows = [thin[2 * h], thin[2 * h + 1], thin[2 * h + 2], jnp.zeros((8, N), F32)]
        high, low = halves(jnp.concatenate(rows, axis=0))
        thin_high[h] = high
        thin_low[h] = low


def taps_one(h, field, thin):
    return jnp.concatenate([field[2 * h], field[2 * h + 1], field[2 * h + 2], thin[h]], axis=0)


def taps_two(h, act):
    return jnp.concatenate([act[2 * h], act[2 * h + 1], act[2 * h + 2]], axis=0)


def beside(function, p, *refs):
    return jnp.concatenate([function(2 * p, *refs), function(2 * p + 1, *refs)], axis=1)


def first_layer(field_high, field_low, thin_high, thin_low, left_one, pre, act):
    def pair(p, carry):
        both = dot(left_one[...], beside(taps_one, p, field_high, thin_high))
        out = both[:N] + both[N:] + dot(left_one[:N, :], beside(taps_one, p, field_low, thin_low))
        active = out / (1.0 + jnp.exp(-out))
        for k in range(2):
            pre[2 * p + k] = out[:, k * N : (k + 1) * N]
            act[2 * p + k] = active[:, k * N : (k + 1) * N]
        return carry

    lax.fori_loop(0, ROWS // 4, pair, 0)


def first_gradient(field_high, field_low, thin_high, thin_low, pre, grad_act):
    def row(h, g, lower):
        value = pre[h]
        s = 1.0 / (1.0 + jnp.exp(-value))
        return grad_act[g, lower * N : (lower + 1) * N, :] * (s * (1.0 + value * (1.0 - s)))

    def pair(p, total):
        grad = jnp.concatenate([row(2 * p, p, 0), row(2 * p + 1, p, 1)], axis=1)
        high, low = halves(grad)
        field = beside(taps_one, p, field_high, thin_high)
        both = dot_nt(jnp.concatenate([high, low], axis=0), field)
        return total + (both[:N] + both[N:]) + dot_nt(high, beside(taps_one, p, field_low, thin_low))

    return lax.fori_loop(0, ROWS // 4, pair, jnp.zeros((N, 4 * N), F32))


def activation_edges(act, edge_ref):
    packed = jnp.zeros((CH, N), F32)
    for y in range(ROWS // 2):
        packed = pack_column(packed, y, act[y, CH:, N - 1 :])
    edge_ref[...] = packed


def split_activation(lat, act, north, from_west, from_corner, high_ref, low_ref):
    def one(place, value, column):
        high, low = halves(jnp.concatenate([enter_west(value[CH:], column), value], axis=0))
        high_ref[place] = high
        low_ref[place] = low

    for y in range(ROWS // 2):
        one(y + 1, act[y], from_west[:, y : y + 1])
    last = ROWS // 2 - 1
    one(0, jnp.where(lat > 0, north[...], 0.0), jnp.where(lat > 0, from_corner[:, last : last + 1], 0.0))


def second_layer(act_high, act_low, left_two, cot, wide_features):
    total = jnp.zeros((CH, 9 * CH), F32)
    for p in range(4):
        high, low = beside(taps_two, p, act_high), beside(taps_two, p, act_low)
        both = dot(left_two[...], high)
        out = both[:CH] + both[CH:] + dot(left_two[:CH, :], low)
        for k in range(2):
            wide_features[:, 2 * p + k, :] = out[:, k * N : (k + 1) * N]
        grad = jnp.concatenate([cot[2 * p], cot[2 * p + 1]], axis=1).astype(BF16)
        total = total + (dot_nt(grad, high) + dot_nt(grad, low))
    return total


def pack_gradients(one, two, part_ref):
    lane = lax.broadcasted_iota(jnp.int32, (CH, 4 * N), 1)
    upper, lower = one[:CH], one[CH:]
    moved = jnp.where(lane < 3 * STEP_ONE, pltpu.roll(lower, 4 * N - 2 * C_OBS, 1), pltpu.roll(lower, 4 * N - 2, 1))
    both = upper + moved
    tight = jnp.where(
        lane < 96, both,
        jnp.where(
            lane < 192, pltpu.roll(both, 4 * N - 64, 1),
            jnp.where(lane < 288, pltpu.roll(both, 4 * N - 128, 1), pltpu.roll(both, 4 * N - 192, 1)),
        ),
    )
    shifted = pltpu.roll(tight, CH, 1)
    part_ref[:, 4 * N : 7 * N] = shifted[:, : 3 * N]
    part_ref[:, : 9 * CH] = two


def unpack_gradients(total_ref, one_ref, two_ref):
    for i in range(9):
        two_ref[i] = total_ref[:, i * CH : (i + 1) * CH]
    turned = total_ref[:, 4 * N : 7 * N].T
    for i in range(9):
        one_ref[i, :C_OBS, :] = turned[CH + i * C_OBS : CH + (i + 1) * C_OBS]
        thin = CH + 9 * C_OBS + (i // 3) * 8 + i % 3
        one_ref[i, C_OBS:, :] = turned[thin : thin + 1]


def phase_picker():
    lane = jnp.arange(4 * N, dtype=jnp.int32)
    source = 4 * (lane % 32) + lane // N
    return (jnp.arange(N, dtype=jnp.int32)[:, None] == source[None, :]).astype(BF16)


class Named:
    def __init__(self, names, refs):
        self.__dict__.update(zip(names, refs))


SCRATCH = {
    "wide": pltpu.VMEM((CAP, C_OBS, N), F32),
    "turned": pltpu.VMEM((N, 16, N), F32),
    "packed": pltpu.VMEM((N, 16, N), BF16),
    "codes": pltpu.VMEM((N, 1, N), jnp.int32),
    "got_w": pltpu.VMEM((N, CAP, N), BF16),
    "got_v": pltpu.VMEM((N, 16, N), BF16),
    "got_c": pltpu.VMEM((N, 1, N), jnp.int32),
    "lhs": pltpu.VMEM((ROWS * C_OBS + ROWS, SLOTS), BF16),
    "rhs": pltpu.VMEM((SLOTS, 4 * N), BF16),
    "acc": pltpu.VMEM((ROWS * C_OBS + ROWS, 4 * N), F32),
    "wide_one": pltpu.VMEM((4 * N, N), F32),
    "wide_adj": pltpu.VMEM((256, 256), F32),
    "wide_two": pltpu.VMEM((CH, 9 * CH), F32),
    "left_one": pltpu.VMEM((256, 4 * N), BF16),
    "left_adj": pltpu.VMEM((512, 256), BF16),
    "left_two": pltpu.VMEM((N, 9 * CH), BF16),
    "wide_cot": pltpu.VMEM((CH, 8, N), F32),
    "cot": pltpu.VMEM((9, CH, N), F32),
    "cot_right": pltpu.VMEM((9, CH, N), F32),
    "cot_col": pltpu.VMEM((CH, N), F32),
    "cot_south": pltpu.VMEM((CH, N), F32),
    "cot_east": pltpu.VMEM((CH, N), F32),
    "cot_corner": pltpu.VMEM((CH, N), F32),
    "grad_act": pltpu.VMEM((8, 256, N), F32),
    "edge": pltpu.VMEM((2 * C_OBS, N), F32),
    "edge_west": pltpu.VMEM((2 * C_OBS, N), F32),
    "edge_corner": pltpu.VMEM((2 * C_OBS, N), F32),
    "north": pltpu.VMEM((C_OBS, 4 * N), F32),
    "north_thin": pltpu.VMEM((8, 4 * N), F32),
    "thin": pltpu.VMEM((ROWS + 1, 8, N), F32),
    "field_high": pltpu.VMEM((ROWS + 1, STEP_ONE, N), BF16),
    "field_low": pltpu.VMEM((ROWS + 1, STEP_ONE, N), BF16),
    "thin_high": pltpu.VMEM((ROWS // 2, 32, N), BF16),
    "thin_low": pltpu.VMEM((ROWS // 2, 32, N), BF16),
    "pre": pltpu.VMEM((ROWS // 2, N, N), F32),
    "act": pltpu.VMEM((ROWS // 2, N, N), F32),
    "act_edge": pltpu.VMEM((CH, N), F32),
    "act_west": pltpu.VMEM((CH, N), F32),
    "act_corner": pltpu.VMEM((CH, N), F32),
    "act_north": pltpu.VMEM((N, N), F32),
    "act_high": pltpu.VMEM((ROWS // 2 + 1, STEP_TWO, N), BF16),
    "act_low": pltpu.VMEM((ROWS // 2 + 1, STEP_TWO, N), BF16),
    "wide_features": pltpu.VMEM((CH, 8, N), F32),
    "part": pltpu.VMEM((CH, 7 * N), F32),
    "total": pltpu.VMEM((CH, 7 * N), F32),
    "by_lat": pltpu.VMEM((8, 8, 7 * N), F32),
    "by_y": pltpu.VMEM((4, 8, 7 * N), F32),
    "by_x": pltpu.VMEM((4, 8, 7 * N), F32),
    "sent": pltpu.SemaphoreType.DMA((3,)),
    "came_w": pltpu.SemaphoreType.DMA((STEPS,)),
    "came_v": pltpu.SemaphoreType.DMA((STEPS,)),
    "came_c": pltpu.SemaphoreType.DMA((STEPS,)),
    "own": pltpu.SemaphoreType.DMA((3,)),
    "halo_sent": pltpu.SemaphoreType.DMA((10,)),
    "halo_came": pltpu.SemaphoreType.DMA((10,)),
    "sum_sent": pltpu.SemaphoreType.DMA((24,)),
    "sum_came": pltpu.SemaphoreType.DMA((24,)),
}


def whole_kernel(
    values_ref, w_ref, blocks_ref, counts_ref, perm_ref, one_ref, two_ref, cot_ref,
    features_ref, grad_one_ref, grad_two_ref, *scratch,
):
    m = Named(SCRATCH, scratch)
    lat, lon = position()
    me = lat * 16 + lon
    barrier = greet_all(lat, lon)
    pack_values(values_ref, m.wide, m.turned, m.packed)
    pack_codes(blocks_ref, counts_ref, m.codes)
    arrange_cotangent(cot_ref, m.wide_cot, m.cot, m.cot_col)
    arrange_kernels(one_ref, two_ref, m.wide_one, m.wide_adj, m.wide_two, m.left_one, m.left_adj, m.left_two)
    m.acc[...] = jnp.zeros_like(m.acc)
    mine = [
        pltpu.make_async_copy(w_ref.at[me], m.got_w.at[0], m.own.at[0]),
        pltpu.make_async_copy(m.packed.at[me], m.got_v.at[0], m.own.at[1]),
        pltpu.make_async_copy(m.codes.at[me], m.got_c.at[0], m.own.at[2]),
    ]
    for copy in mine:
        copy.start()

    north, south = lax.rem(lat + 7, 8), lax.rem(lat + 1, 8)
    west, east = lax.rem(lon + 15, 16), lax.rem(lon + 1, 16)

    def halo(k, source, target, device):
        return send_to(source, target, m.halo_sent.at[k], m.halo_came.at[k], device)

    cot_halo = [
        halo(0, m.cot_col, m.cot_east, (lat, west)),
        halo(1, m.cot.at[0], m.cot_south, (north, lon)),
        halo(2, m.cot_col, m.cot_corner, (north, west)),
    ]
    pl.semaphore_wait(barrier, N - 1)
    for copy in cot_halo:
        copy.start()

    streams = ((w_ref, m.got_w, m.came_w), (m.packed, m.got_v, m.came_v), (m.codes, m.got_c, m.came_c))

    def send(ordinal, carry):
        to_lat, to_lon = partner(lat, lon, ordinal, 1)
        to = to_lat * 16 + to_lon
        step = ordinal // GROUP
        for k, (source, target, came) in enumerate(streams):
            send_to(source.at[to], target.at[ordinal], m.sent.at[k], came.at[step], (to_lat, to_lon)).start()
        return carry

    lax.fori_loop(1, N, send, 0)
    for copy in cot_halo:
        copy.wait()
    back_to_activation(
        lat, m.cot, m.cot_south, m.cot_east, m.cot_corner, m.cot_right, m.left_adj, m.grad_act
    )
    for copy in mine:
        copy.wait()

    def arrive(first, count, step):
        for source, target, came in streams:
            pltpu.make_async_copy(
                target.at[pl.ds(first, count)], target.at[pl.ds(first, count)], came.at[step]
            ).wait()

    def work(step, carry):
        @pl.when(step == 0)
        def _():
            arrive(1, GROUP - 1, 0)

        @pl.when(step > 0)
        def _():
            arrive(step * GROUP, GROUP, step)

        spread_group(step, m.got_w, m.got_v, m.got_c, perm_ref, m.lhs, m.rhs, m.acc)
        return carry

    lax.fori_loop(0, STEPS, work, 0)

    last = ROWS * C_OBS
    rows_halo = [
        halo(3, m.acc.at[pl.ds(last - C_OBS, C_OBS)], m.north, (south, lon)),
        halo(4, m.acc.at[pl.ds(last + ROWS - 8, 8)], m.north_thin, (south, lon)),
    ]
    edge_halo = [
        halo(5, m.edge, m.edge_west, (lat, east)),
        halo(6, m.edge, m.edge_corner, (south, east)),
    ]
    for copy in rows_halo:
        copy.start()
    field_edges(m.acc, m.edge)
    for copy in edge_halo:
        copy.start()
    for copy in edge_halo + rows_halo:
        copy.wait()
    split_field(
        lat, m.acc, m.north, m.north_thin, m.edge_west, m.edge_corner, m.thin,
        m.field_high, m.field_low, m.thin_high, m.thin_low,
    )
    field = (m.field_high, m.field_low, m.thin_high, m.thin_low)
    first_layer(*field, m.left_one, m.pre, m.act)
    act_halo = [
        halo(7, m.act.at[ROWS // 2 - 1], m.act_north, (south, lon)),
        halo(8, m.act_edge, m.act_west, (lat, east)),
        halo(9, m.act_edge, m.act_corner, (south, east)),
    ]
    act_halo[0].start()
    activation_edges(m.act, m.act_edge)
    act_halo[1].start()
    act_halo[2].start()
    grad_one = first_gradient(*field, m.pre, m.grad_act)
    for copy in act_halo:
        copy.wait()
    split_activation(lat, m.act, m.act_north, m.act_west, m.act_corner, m.act_high, m.act_low)
    grad_two = second_layer(m.act_high, m.act_low, m.left_two, m.cot, m.wide_features)
    pack_gradients(grad_one, grad_two, m.part)
    features_ref[...] = m.wide_features[...].astype(BF16)
    all_sum(lat, lon, m.part, m.total, m.by_lat, m.by_y, m.by_x, m.sum_sent, m.sum_came)
    unpack_gradients(m.total, grad_one_ref, grad_two_ref)
    for k, (_, target, _) in enumerate(streams):
        pltpu.make_async_copy(target.at[pl.ds(0, N - 1)], target.at[pl.ds(0, N - 1)], m.sent.at[k]).wait()


def on_device(
    obs_values, kernel_weights, pixel_blocks, obs_counts, kernel_one, kernel_two, cotangent
):
    vmem = pl.BlockSpec(memory_space=pltpu.VMEM)
    features, grad_one, grad_two = pl.pallas_call(
        whole_kernel,
        out_shape=(
            jax.ShapeDtypeStruct((CH, 8, N), BF16),
            jax.ShapeDtypeStruct((9, C_OBS + 1, CH), F32),
            jax.ShapeDtypeStruct((9, CH, CH), F32),
        ),
        in_specs=[vmem, pl.BlockSpec(memory_space=pl.ANY)] + [vmem] * 6,
        out_specs=(vmem, vmem, vmem),
        scratch_shapes=list(SCRATCH.values()),
        compiler_params=pltpu.CompilerParams(collective_id=0, has_side_effects=True, vmem_limit_bytes=56 << 20),
    )(
        obs_values[0].transpose(1, 2, 0),
        kernel_weights[0],
        pixel_blocks[0].T,
        obs_counts,
        phase_picker(),
        kernel_one.transpose(0, 1, 3, 2),
        kernel_two,
        cotangent,
    )
    grad_one = grad_one.reshape(3, 3, C_OBS + 1, CH).transpose(0, 1, 3, 2)
    return features, grad_one, grad_two.reshape(3, 3, CH, CH)


def solution(mesh):
    placed = (
        P(("lat", "lon"), None, None, None),
        P(("lat", "lon"), None, None, None),
        P(("lat", "lon"), None, None),
        P(("lat", "lon"), None),
        P(),
        P(),
        P(None, "lat", "lon"),
    )
    return jax.shard_map(
        on_device,
        mesh=mesh,
        in_specs=placed,
        out_specs=(P(None, "lat", "lon"), P(), P()),
        check_vma=False,
    )
```

```python
import jax
import jax.numpy as jnp
from jax import lax
from jax.experimental import pallas as pl
from jax.experimental.pallas import tpu as pltpu
from jax.sharding import PartitionSpec as P

MESH = pl.DeviceIdType.MESH
F32, BF16 = jnp.float32, jnp.bfloat16
N = 128
CAP = 64
GROUP = 16
STEPS = N // GROUP - 1
SLOTS = GROUP * CAP
SENT = CAP + 16
ROWS = 32
C_OBS = 32


def position():
    return lax.axis_index("lat"), lax.axis_index("lon")


def partner(lat, lon, ordinal):
    mixed = lax.rem(ordinal * 37, N)
    z = lax.rem(lat // 2 + lax.rem(mixed // 2, 4), 4)
    core = lax.rem(lat + lax.rem(mixed, 2), 2)
    x = lax.rem(lon // 4 + lax.rem(mixed // 8, 4), 4)
    y = lax.rem(lon + mixed // 32, 4)
    return z * 2 + core, x * 4 + y


NEAR = 22


def greet_near(lat, lon):
    barrier = pltpu.get_barrier_semaphore()
    for d in range(1, 16):
        pl.semaphore_signal(barrier, inc=1, device_id=(lat, lax.rem(lon + d, 16)), device_id_type=MESH)
    for d in range(1, 8):
        pl.semaphore_signal(barrier, inc=1, device_id=(lax.rem(lat + d, 8), lon), device_id_type=MESH)
    return barrier


def pack_values(wide_ref, turned_ref, message_ref):
    for i in range(16):
        pair = jnp.concatenate([wide_ref[:, i, :], wide_ref[:, 16 + i, :]], axis=0)
        turned_ref[:, i, :] = pair.T
    message_ref[:, CAP:, :] = turned_ref[...].astype(BF16)


def pack_codes(blocks_ref, counts_ref, codes_ref):
    slot = lax.broadcasted_iota(jnp.int32, (CAP, N), 0)
    code = jnp.where(slot < counts_ref[...], blocks_ref[...], 4 * ROWS)
    turned = jnp.concatenate([code, code], axis=0).astype(F32).T.astype(jnp.int32)
    codes_ref[:, 0, :] = turned


def spread_group(first, group, got, got_c, perm_ref, lhs_ref, rhs_ref, acc_ref):
    slots = group * CAP
    lane = lax.broadcasted_iota(jnp.int32, (1, N), 1)
    codes = got_c[pl.ds(first, group), 0, :]
    row_parts, value_parts = [], []
    for p in range(group // 2):
        even, odd = codes[2 * p : 2 * p + 1], codes[2 * p + 1 : 2 * p + 2]
        row_parts.append(jnp.where(lane < CAP, even, odd))
        one = got[first + 2 * p, CAP:, :].astype(F32)
        two = got[first + 2 * p + 1, CAP:, :].astype(F32)
        upper = jnp.where(lane < CAP, one, pltpu.roll(two, CAP, 1))
        lower = jnp.where(lane < CAP, pltpu.roll(one, CAP, 1), two)
        value_parts.append(jnp.concatenate([upper, lower], axis=0))
    row_of = jnp.broadcast_to(jnp.concatenate(row_parts, axis=1) // 4, (C_OBS, slots)).astype(F32).astype(BF16)
    values = jnp.concatenate(value_parts, axis=1).astype(BF16)
    zero = jnp.zeros_like(values)
    for r in range(ROWS):
        lhs_ref[r * C_OBS : (r + 1) * C_OBS, :slots] = jnp.where(row_of == jnp.array(r, BF16), values, zero)
    rows = lax.broadcasted_iota(jnp.int32, (ROWS, slots), 0).astype(F32).astype(BF16)
    lhs_ref[ROWS * C_OBS :, :slots] = jnp.where(row_of == rows, jnp.ones_like(values), zero)
    quarter = lax.rem(codes, 4).astype(F32).T
    lane_quarter = (lax.broadcasted_iota(jnp.int32, (CAP, N), 1) // 32).astype(F32)
    for s in range(group):
        keep = jnp.where(quarter[:CAP, s : s + 1] == lane_quarter, 1.0, 0.0).astype(BF16)
        pixels = jnp.dot(got[first + s, :CAP, :], perm_ref[...], preferred_element_type=F32).astype(BF16)
        for phase in range(4):
            rhs_ref[s * CAP : (s + 1) * CAP, phase * N : (phase + 1) * N] = (
                pixels[:, phase * N : (phase + 1) * N] * keep
            )
    acc_ref[...] += jnp.dot(lhs_ref[:, :slots], rhs_ref[:slots, :], preferred_element_type=F32)


def send_to(source, target, sent, came, device):
    return pltpu.make_async_remote_copy(
        src_ref=source, dst_ref=target, send_sem=sent, recv_sem=came, device_id=device, device_id_type=MESH
    )


def all_sum(lat, lon, part_ref, total_ref, by_lon, by_lat, sent, came):
    def piece(ref, p):
        rows = pl.ds(pl.multiple_of(8 * (p // 2), 8), 8)
        return ref.at[rows, pl.ds(pl.multiple_of(512 * lax.rem(p, 2), 512), 512)]

    copies = []
    for d in range(1, 16):
        to = lax.rem(lon + d, 16)
        copies.append(send_to(piece(part_ref, to), by_lon.at[d], sent.at[d], came.at[d], (lat, to)))
    for copy in copies:
        copy.start()
    total = piece(part_ref, lon)[...]
    for d in range(1, 16):
        copies[d - 1].wait()
        total = total + by_lon[d]
    by_lat[lat] = total
    copies = []
    for d in range(1, 8):
        to = lax.rem(lat + d, 8)
        copies.append(send_to(by_lat.at[lat], by_lat.at[lat], sent.at[16 + d], came.at[16 + d], (to, lon)))
    for copy in copies:
        copy.start()
    for copy in copies:
        copy.wait()
    total = by_lat[0]
    for d in range(1, 8):
        total = total + by_lat[d]
    mine = piece(total_ref, lon)
    mine[...] = total
    copies = []
    for d in range(1, 16):
        copies.append(send_to(mine, mine, sent.at[24 + d], came.at[24 + d], (lat, lax.rem(lon + d, 16))))
    for copy in copies:
        copy.start()
    for copy in copies:
        copy.wait()


CH = 64
STEP_ONE = 5 * C_OBS
STEP_TWO = 3 * CH


def halves(value):
    high = value.astype(BF16)
    return high, (value - high.astype(F32)).astype(BF16)


def dot_nt(a, b):
    return lax.dot_general(a, b, (((1,), (1,)), ((), ())), preferred_element_type=F32)


def dot(a, b):
    return jnp.dot(a, b, preferred_element_type=F32)


def lanes(rows):
    return lax.broadcasted_iota(jnp.int32, (rows, N), 1)


def pack_column(total, place, column):
    return jnp.where(lanes(total.shape[0]) == place, jnp.broadcast_to(column, total.shape), total)


def enter_west(value, column):
    moved = pltpu.roll(value, 1, 1)
    return jnp.where(lanes(value.shape[0]) == 0, jnp.broadcast_to(column, value.shape), moved)


def enter_east(value, column):
    moved = pltpu.roll(value, N - 1, 1)
    return jnp.where(lanes(value.shape[0]) == N - 1, jnp.broadcast_to(column, value.shape), moved)


def arrange_kernels(one_ref, two_ref, wide_one, wide_adj, wide_two, left_one, left_adj, left_two):
    wide_one[...] = jnp.zeros_like(wide_one)
    wide_adj[...] = jnp.zeros_like(wide_adj)
    for a in range(3):
        for tap in range(5):
            row = a * STEP_ONE + tap * C_OBS
            thin = 3 * STEP_ONE + a * 8 + tap
            for half, e in ((0, tap), (1, tap - 2)):
                if 0 <= e < 3:
                    at = slice(half * CH, half * CH + CH)
                    wide_one[row : row + C_OBS, at] = one_ref[a, e, :C_OBS, :]
                    wide_one[thin : thin + 1, at] = one_ref[a, e, C_OBS:, :]
        for e in range(3):
            at = (a * 3 + e) * CH
            wide_two[:, at : at + CH] = two_ref[a, e]
    for lower in range(2):
        for east in range(2):
            for down in range(lower + 1):
                for right in range(east + 1):
                    a = 1 if lower == 0 else 2 - 2 * down
                    e = 1 if east == 0 else 2 - 2 * right
                    row, col = (down * 2 + right) * CH, (lower * 2 + east) * CH
                    wide_adj[row : row + CH, col : col + CH] = two_ref[a, e]
    for wide, left, turn in ((wide_one, left_one, True), (wide_adj, left_adj, True), (wide_two, left_two, False)):
        value = wide[...].T if turn else wide[...]
        high, low = halves(value)
        rows = value.shape[0]
        left[:rows, :] = high
        left[rows:, :] = low


def arrange_cotangent(cot_ref, wide_cot, cot, cot_col):
    wide_cot[...] = cot_ref[...].astype(F32)
    packed = jnp.zeros((CH, N), F32)
    for g in range(8):
        value = wide_cot[:, g, :]
        cot[g] = value
        packed = pack_column(packed, g, value[:, :1])
    cot_col[...] = packed


def back_to_activation(lat, cot, from_south, from_east, from_corner, right, left_adj, grad_act):
    cot[8] = jnp.where(lat < 7, from_south[...], 0.0)
    edge = from_east[...]
    for g in range(9):
        column = edge[:, g : g + 1] if g < 8 else jnp.where(lat < 7, from_corner[:, :1], 0.0)
        right[g] = enter_east(cot[g], column)

    def pair(p, carry):
        stack = [
            jnp.concatenate([cot[g], right[g], cot[g + 1], right[g + 1]], axis=0).astype(BF16)
            for g in (2 * p, 2 * p + 1)
        ]
        both = dot(left_adj[...], jnp.concatenate(stack, axis=1))
        both = both[:256] + both[256:]
        grad_act[2 * p] = both[:, :N]
        grad_act[2 * p + 1] = both[:, N:]
        return carry

    lax.fori_loop(0, 4, pair, 0)


def field_edges(acc_ref, edge_ref):
    packed = jnp.zeros((C_OBS, N), F32)
    for r in range(ROWS):
        packed = pack_column(packed, r, acc_ref[r * C_OBS : (r + 1) * C_OBS, 4 * N - 1 :])
    edge_ref[:C_OBS, :] = packed
    edge_ref[C_OBS:, :] = acc_ref[ROWS * C_OBS :, 3 * N :]


def split_inside(acc_ref, thin, high_ref, low_ref):
    for r in range(ROWS):
        for phase in range(4):
            high, low = halves(acc_ref[r * C_OBS : (r + 1) * C_OBS, phase * N : (phase + 1) * N])
            at = slice((phase + 1) * C_OBS, (phase + 2) * C_OBS)
            high_ref[r + 1, at, :] = high
            low_ref[r + 1, at, :] = low
    thin[...] = jnp.zeros_like(thin)
    for phase in range(4):
        thin[1 : ROWS + 1, phase + 1, :] = acc_ref[ROWS * C_OBS :, phase * N : (phase + 1) * N]


def split_rim(lat, acc_ref, north, north_thin, from_west, from_corner, thin, high_ref, low_ref, thin_high, thin_low):
    for r in range(ROWS):
        moved = enter_west(acc_ref[r * C_OBS : (r + 1) * C_OBS, 3 * N :], from_west[:C_OBS, r : r + 1])
        high, low = halves(moved)
        high_ref[r + 1, :C_OBS, :] = high
        low_ref[r + 1, :C_OBS, :] = low
    inside = lat > 0
    phases = [jnp.where(inside, north[:, phase * N : (phase + 1) * N], 0.0) for phase in range(4)]
    corner = jnp.where(inside, from_corner[:C_OBS, ROWS - 1 : ROWS], 0.0)
    high, low = halves(jnp.concatenate([enter_west(phases[3], corner)] + phases, axis=0))
    high_ref[0] = high
    low_ref[0] = low
    for phase in range(4):
        at = slice(phase * N, (phase + 1) * N)
        thin[0, phase + 1 : phase + 2, :] = jnp.where(inside, north_thin[7:8, at], 0.0)
    thin[1 : ROWS + 1, 0, :] = enter_west(acc_ref[ROWS * C_OBS :, 3 * N :], from_west[C_OBS:, N - 1 :])
    corner = enter_west(north_thin[7:8, 3 * N :], from_corner[2 * C_OBS - 1 :, N - 1 :])
    thin[0, 0:1, :] = jnp.where(inside, corner, 0.0)
    for h in range(ROWS // 2):
        rows = [thin[2 * h], thin[2 * h + 1], thin[2 * h + 2], jnp.zeros((8, N), F32)]
        high, low = halves(jnp.concatenate(rows, axis=0))
        thin_high[h] = high
        thin_low[h] = low


def taps_one(h, field, thin):
    return jnp.concatenate([field[2 * h], field[2 * h + 1], field[2 * h + 2], thin[h]], axis=0)


def taps_two(h, act):
    return jnp.concatenate([act[2 * h], act[2 * h + 1], act[2 * h + 2]], axis=0)


def beside(function, p, *refs):
    return jnp.concatenate([function(2 * p, *refs), function(2 * p + 1, *refs)], axis=1)


def first_layer(field_high, field_low, thin_high, thin_low, left_one, pre, act):
    def pair(p, carry):
        both = dot(left_one[...], beside(taps_one, p, field_high, thin_high))
        out = both[:N] + both[N:] + dot(left_one[:N, :], beside(taps_one, p, field_low, thin_low))
        active = out / (1.0 + jnp.exp(-out))
        for k in range(2):
            pre[2 * p + k] = out[:, k * N : (k + 1) * N]
            act[2 * p + k] = active[:, k * N : (k + 1) * N]
        return carry

    lax.fori_loop(0, ROWS // 4, pair, 0)


def first_gradient(field_high, field_low, thin_high, thin_low, pre, grad_act):
    def row(h, g, lower):
        value = pre[h]
        s = 1.0 / (1.0 + jnp.exp(-value))
        return grad_act[g, lower * N : (lower + 1) * N, :] * (s * (1.0 + value * (1.0 - s)))

    def pair(p, total):
        grad = jnp.concatenate([row(2 * p, p, 0), row(2 * p + 1, p, 1)], axis=1)
        high, low = halves(grad)
        field = beside(taps_one, p, field_high, thin_high)
        both = dot_nt(jnp.concatenate([high, low], axis=0), field)
        return total + (both[:N] + both[N:]) + dot_nt(high, beside(taps_one, p, field_low, thin_low))

    return lax.fori_loop(0, ROWS // 4, pair, jnp.zeros((N, 4 * N), F32))


def activation_edges(act, edge_ref):
    packed = jnp.zeros((CH, N), F32)
    for y in range(ROWS // 2):
        packed = pack_column(packed, y, act[y, CH:, N - 1 :])
    edge_ref[...] = packed


def split_activation(lat, act, north, from_west, from_corner, high_ref, low_ref):
    def one(place, value, column):
        high, low = halves(jnp.concatenate([enter_west(value[CH:], column), value], axis=0))
        high_ref[place] = high
        low_ref[place] = low

    for y in range(ROWS // 2):
        one(y + 1, act[y], from_west[:, y : y + 1])
    last = ROWS // 2 - 1
    one(0, jnp.where(lat > 0, north[...], 0.0), jnp.where(lat > 0, from_corner[:, last : last + 1], 0.0))


def second_layer(act_high, act_low, left_two, cot, wide_features):
    total = jnp.zeros((CH, 9 * CH), F32)
    for p in range(4):
        high, low = beside(taps_two, p, act_high), beside(taps_two, p, act_low)
        both = dot(left_two[...], high)
        out = both[:CH] + both[CH:] + dot(left_two[:CH, :], low)
        for k in range(2):
            wide_features[:, 2 * p + k, :] = out[:, k * N : (k + 1) * N]
        grad = jnp.concatenate([cot[2 * p], cot[2 * p + 1]], axis=1).astype(BF16)
        total = total + (dot_nt(grad, high) + dot_nt(grad, low))
    return total


def pack_gradients(one, two, part_ref):
    lane = lax.broadcasted_iota(jnp.int32, (CH, 4 * N), 1)
    upper, lower = one[:CH], one[CH:]
    moved = jnp.where(lane < 3 * STEP_ONE, pltpu.roll(lower, 4 * N - 2 * C_OBS, 1), pltpu.roll(lower, 4 * N - 2, 1))
    both = upper + moved
    tight = jnp.where(
        lane < 96, both,
        jnp.where(
            lane < 192, pltpu.roll(both, 4 * N - 64, 1),
            jnp.where(lane < 288, pltpu.roll(both, 4 * N - 128, 1), pltpu.roll(both, 4 * N - 192, 1)),
        ),
    )
    shifted = pltpu.roll(tight, CH, 1)
    part_ref[:, 4 * N :] = shifted
    part_ref[:, : 9 * CH] = two


def unpack_gradients(total_ref, one_ref, two_ref):
    for i in range(9):
        two_ref[i] = total_ref[:, i * CH : (i + 1) * CH]
    turned = total_ref[:, 4 * N : 7 * N].T
    for i in range(9):
        one_ref[i, :C_OBS, :] = turned[CH + i * C_OBS : CH + (i + 1) * C_OBS]
        thin = CH + 9 * C_OBS + (i // 3) * 8 + i % 3
        one_ref[i, C_OBS:, :] = turned[thin : thin + 1]


def arrange_picker(picker_ref):
    lane = lax.broadcasted_iota(jnp.int32, (N, 4 * N), 1)
    pixel = lax.broadcasted_iota(jnp.int32, (N, 4 * N), 0)
    picker_ref[...] = jnp.where(pixel == 4 * lax.rem(lane, 32) + lane // N, 1.0, 0.0).astype(BF16)


class Named:
    def __init__(self, names, refs):
        self.__dict__.update(zip(names, refs))


SCRATCH = {
    "wide": pltpu.VMEM((CAP, C_OBS, N), F32),
    "turned": pltpu.VMEM((N, 16, N), F32),
    "codes": pltpu.VMEM((N, 1, N), jnp.int32),
    "got_codes": pltpu.VMEM((N, 1, N), jnp.int32),
    "message": pltpu.VMEM((N, SENT, N), BF16),
    "got": pltpu.VMEM((N, SENT, N), BF16),
    "lhs": pltpu.VMEM((ROWS * C_OBS + ROWS, SLOTS), BF16),
    "rhs": pltpu.VMEM((SLOTS, 4 * N), BF16),
    "acc": pltpu.VMEM((ROWS * C_OBS + ROWS, 4 * N), F32),
    "wide_one": pltpu.VMEM((4 * N, N), F32),
    "wide_adj": pltpu.VMEM((256, 256), F32),
    "wide_two": pltpu.VMEM((CH, 9 * CH), F32),
    "left_one": pltpu.VMEM((256, 4 * N), BF16),
    "left_adj": pltpu.VMEM((512, 256), BF16),
    "left_two": pltpu.VMEM((N, 9 * CH), BF16),
    "wide_cot": pltpu.VMEM((CH, 8, N), F32),
    "cot": pltpu.VMEM((9, CH, N), F32),
    "cot_right": pltpu.VMEM((9, CH, N), F32),
    "cot_col": pltpu.VMEM((CH, N), F32),
    "cot_south": pltpu.VMEM((CH, N), F32),
    "cot_east": pltpu.VMEM((CH, N), F32),
    "cot_corner": pltpu.VMEM((CH, N), F32),
    "grad_act": pltpu.VMEM((8, 256, N), F32),
    "edge": pltpu.VMEM((2 * C_OBS, N), F32),
    "edge_west": pltpu.VMEM((2 * C_OBS, N), F32),
    "edge_corner": pltpu.VMEM((2 * C_OBS, N), F32),
    "north": pltpu.VMEM((C_OBS, 4 * N), F32),
    "north_thin": pltpu.VMEM((8, 4 * N), F32),
    "thin": pltpu.VMEM((ROWS + 1, 8, N), F32),
    "field_high": pltpu.VMEM((ROWS + 1, STEP_ONE, N), BF16),
    "field_low": pltpu.VMEM((ROWS + 1, STEP_ONE, N), BF16),
    "thin_high": pltpu.VMEM((ROWS // 2, 32, N), BF16),
    "thin_low": pltpu.VMEM((ROWS // 2, 32, N), BF16),
    "pre": pltpu.VMEM((ROWS // 2, N, N), F32),
    "act": pltpu.VMEM((ROWS // 2, N, N), F32),
    "act_edge": pltpu.VMEM((CH, N), F32),
    "act_west": pltpu.VMEM((CH, N), F32),
    "act_corner": pltpu.VMEM((CH, N), F32),
    "act_north": pltpu.VMEM((N, N), F32),
    "act_high": pltpu.VMEM((ROWS // 2 + 1, STEP_TWO, N), BF16),
    "act_low": pltpu.VMEM((ROWS // 2 + 1, STEP_TWO, N), BF16),
    "grad_one": pltpu.VMEM((9, C_OBS + 1, CH), F32),
    "grad_two": pltpu.VMEM((9, CH, CH), F32),
    "features": pltpu.VMEM((CH, 8, N), BF16),
    "wide_features": pltpu.VMEM((CH, 8, N), F32),
    "part": pltpu.VMEM((CH, 8 * N), F32),
    "total": pltpu.VMEM((CH, 8 * N), F32),
    "by_lon": pltpu.VMEM((16, 8, 4 * N), F32),
    "by_lat": pltpu.VMEM((8, 8, 4 * N), F32),
    "sent": pltpu.SemaphoreType.DMA((2,)),
    "came": pltpu.SemaphoreType.DMA((2, STEPS + 2)),
    "values": pltpu.VMEM((CAP, C_OBS, N), BF16),
    "blocks": pltpu.VMEM((CAP, N), jnp.int32),
    "counts": pltpu.VMEM((1, N), jnp.int32),
    "cot_in": pltpu.VMEM((CH, 8, N), BF16),
    "one": pltpu.VMEM((3, 3, C_OBS + 1, CH), F32),
    "two": pltpu.VMEM((3, 3, CH, CH), F32),
    "picker": pltpu.VMEM((N, 4 * N), BF16),
    "fetch": pltpu.SemaphoreType.DMA((7,)),
    "met": pltpu.SemaphoreType.REGULAR,
    "own": pltpu.SemaphoreType.DMA((2,)),
    "result": pltpu.SemaphoreType.DMA((3,)),
    "halo_sent": pltpu.SemaphoreType.DMA((10,)),
    "halo_came": pltpu.SemaphoreType.DMA((10,)),
    "sum_sent": pltpu.SemaphoreType.DMA((40,)),
    "sum_came": pltpu.SemaphoreType.DMA((40,)),
}


def whole_kernel(
    values_ref, w_ref, blocks_ref, counts_ref, one_ref, two_ref, cot_ref,
    features_ref, grad_one_ref, grad_two_ref, *scratch,
):
    m = Named(SCRATCH, scratch)
    lat, lon = position()
    me = lat * 16 + lon
    barrier = greet_near(lat, lon)
    fetched = [
        pltpu.make_async_copy(source, target, m.fetch.at[k])
        for k, (source, target) in enumerate((
            (values_ref, m.values), (blocks_ref, m.blocks), (counts_ref, m.counts),
            (w_ref, m.message.at[:, pl.ds(0, CAP)]),
            (cot_ref, m.cot_in), (one_ref, m.one), (two_ref, m.two),
        ))
    ]
    for copy in fetched:
        copy.start()
    arrange_picker(m.picker)

    north, south = lax.rem(lat + 7, 8), lax.rem(lat + 1, 8)
    west, east = lax.rem(lon + 15, 16), lax.rem(lon + 1, 16)

    def halo(k, source, target, device):
        return send_to(source, target, m.halo_sent.at[k], m.halo_came.at[k], device)

    pl.semaphore_wait(barrier, NEAR)
    for d in range(1, 16):
        pl.semaphore_signal(m.met, inc=1, device_id=(lat, lax.rem(lon + d, 16)), device_id_type=MESH)
    fetched[0].wait()
    m.wide[...] = m.values[...].astype(F32)
    pack_values(m.wide, m.turned, m.message)
    fetched[1].wait()
    fetched[2].wait()
    pack_codes(m.blocks, m.counts, m.codes)
    fetched[3].wait()
    streams = ((m.message, m.got), (m.codes, m.got_codes))
    mine = [
        pltpu.make_async_copy(source.at[me], target.at[0], m.own.at[k]) for k, (source, target) in enumerate(streams)
    ]
    for copy in mine:
        copy.start()
    def send(ordinal, carry):
        to_lat, to_lon = partner(lat, lon, ordinal)
        step = jnp.where(ordinal < STEPS * GROUP, ordinal // GROUP, ordinal // (GROUP // 2) - STEPS)
        to = to_lat * 16 + to_lon
        for k, (source, target) in enumerate(streams):
            send_to(
                source.at[to], target.at[ordinal], m.sent.at[k], m.came.at[k, step], (to_lat, to_lon)
            ).start()
        return carry

    fetched[4].wait()
    arrange_cotangent(m.cot_in, m.wide_cot, m.cot, m.cot_col)
    cot_halo = [
        halo(0, m.cot_col, m.cot_east, (lat, west)),
        halo(1, m.cot.at[0], m.cot_south, (north, lon)),
        halo(2, m.cot_col, m.cot_corner, (north, west)),
    ]
    cot_halo[0].start()
    cot_halo[1].start()
    pl.semaphore_wait(m.met, 15)
    cot_halo[2].start()
    lax.fori_loop(1, N, send, 0)

    fetched[5].wait()
    fetched[6].wait()
    arrange_kernels(m.one, m.two, m.wide_one, m.wide_adj, m.wide_two, m.left_one, m.left_adj, m.left_two)
    m.acc[...] = jnp.zeros_like(m.acc)
    for copy in cot_halo:
        copy.wait()
    back_to_activation(
        lat, m.cot, m.cot_south, m.cot_east, m.cot_corner, m.cot_right, m.left_adj, m.grad_act
    )
    for copy in mine:
        copy.wait()

    def arrive(first, count, step):
        for k, (_, target) in enumerate(streams):
            part = target.at[pl.ds(first, count)]
            pltpu.make_async_copy(part, part, m.came.at[k, step]).wait()

    def spread(first, group):
        spread_group(first, group, m.got, m.got_codes, m.picker, m.lhs, m.rhs, m.acc)

    def work(step, carry):
        @pl.when(step == 0)
        def _():
            arrive(1, GROUP - 1, 0)

        @pl.when(step > 0)
        def _():
            arrive(step * GROUP, GROUP, step)

        spread(step * GROUP, GROUP)
        return carry

    lax.fori_loop(0, STEPS, work, 0)

    def work_half(step, carry):
        first = STEPS * GROUP + step * (GROUP // 2)
        arrive(first, GROUP // 2, STEPS + step)
        spread(first, GROUP // 2)
        return carry

    lax.fori_loop(0, 2, work_half, 0)

    last = ROWS * C_OBS
    rows_halo = [
        halo(3, m.acc.at[pl.ds(last - C_OBS, C_OBS)], m.north, (south, lon)),
        halo(4, m.acc.at[pl.ds(last + ROWS - 8, 8)], m.north_thin, (south, lon)),
    ]
    edge_halo = [
        halo(5, m.edge, m.edge_west, (lat, east)),
        halo(6, m.edge, m.edge_corner, (south, east)),
    ]
    for copy in rows_halo:
        copy.start()
    field_edges(m.acc, m.edge)
    for copy in edge_halo:
        copy.start()
    split_inside(m.acc, m.thin, m.field_high, m.field_low)
    for copy in edge_halo + rows_halo:
        copy.wait()
    split_rim(
        lat, m.acc, m.north, m.north_thin, m.edge_west, m.edge_corner, m.thin,
        m.field_high, m.field_low, m.thin_high, m.thin_low,
    )
    field = (m.field_high, m.field_low, m.thin_high, m.thin_low)
    first_layer(*field, m.left_one, m.pre, m.act)
    act_halo = [
        halo(7, m.act.at[ROWS // 2 - 1], m.act_north, (south, lon)),
        halo(8, m.act_edge, m.act_west, (lat, east)),
        halo(9, m.act_edge, m.act_corner, (south, east)),
    ]
    act_halo[0].start()
    activation_edges(m.act, m.act_edge)
    act_halo[1].start()
    act_halo[2].start()
    grad_one = first_gradient(*field, m.pre, m.grad_act)
    for copy in act_halo:
        copy.wait()
    split_activation(lat, m.act, m.act_north, m.act_west, m.act_corner, m.act_high, m.act_low)
    grad_two = second_layer(m.act_high, m.act_low, m.left_two, m.cot, m.wide_features)
    pack_gradients(grad_one, grad_two, m.part)
    m.features[...] = m.wide_features[...].astype(BF16)
    results = [
        pltpu.make_async_copy(m.features, features_ref, m.result.at[0]),
        pltpu.make_async_copy(m.grad_one, grad_one_ref, m.result.at[1]),
        pltpu.make_async_copy(m.grad_two, grad_two_ref, m.result.at[2]),
    ]
    results[0].start()
    all_sum(lat, lon, m.part, m.total, m.by_lon, m.by_lat, m.sum_sent, m.sum_came)
    unpack_gradients(m.total, m.grad_one, m.grad_two)
    results[1].start()
    results[2].start()
    for k, (_, target) in enumerate(streams):
        everything = target.at[pl.ds(0, N - 1)]
        pltpu.make_async_copy(everything, everything, m.sent.at[k]).wait()
    for copy in results:
        copy.wait()


def hand_on_kernel(*refs):
    for k in range(3):
        refs[3 + k][...] = refs[k][...]


def on_device(
    obs_values, kernel_weights, pixel_blocks, obs_counts, kernel_one, kernel_two, cotangent
):
    vmem, anywhere = pl.BlockSpec(memory_space=pltpu.VMEM), pl.BlockSpec(memory_space=pl.ANY)
    outputs = (
        jax.ShapeDtypeStruct((CH, 8, N), BF16),
        jax.ShapeDtypeStruct((9, C_OBS + 1, CH), F32),
        jax.ShapeDtypeStruct((9, CH, CH), F32),
    )
    results = pl.pallas_call(
        whole_kernel,
        out_shape=outputs,
        in_specs=[anywhere] * 7,
        out_specs=(anywhere,) * 3,
        scratch_shapes=list(SCRATCH.values()),
        compiler_params=pltpu.CompilerParams(collective_id=0, has_side_effects=True, vmem_limit_bytes=56 << 20),
    )(
        obs_values[0].transpose(1, 2, 0),
        kernel_weights[0],
        pixel_blocks[0].T,
        obs_counts,
        kernel_one.transpose(0, 1, 3, 2),
        kernel_two,
        cotangent,
    )
    features, grad_one, grad_two = pl.pallas_call(
        hand_on_kernel,
        out_shape=outputs,
        in_specs=[vmem] * 3,
        out_specs=(vmem,) * 3,
        scratch_shapes=[pltpu.SemaphoreType.DMA((3,))],
    )(*results)
    grad_one = grad_one.reshape(3, 3, C_OBS + 1, CH).transpose(0, 1, 3, 2)
    return features, grad_one, grad_two.reshape(3, 3, CH, CH)


def solution(mesh):
    placed = (
        P(("lat", "lon"), None, None, None),
        P(("lat", "lon"), None, None, None),
        P(("lat", "lon"), None, None),
        P(("lat", "lon"), None),
        P(),
        P(),
        P(None, "lat", "lon"),
    )
    return jax.shard_map(
        on_device,
        mesh=mesh,
        in_specs=placed,
        out_specs=(P(None, "lat", "lon"), P(), P()),
        check_vma=False,
    )
```

```python
import jax
import jax.numpy as jnp
from jax import lax
from jax.experimental import pallas as pl
from jax.experimental.pallas import tpu as pltpu
from jax.sharding import PartitionSpec as P

MESH = pl.DeviceIdType.MESH
F32, BF16 = jnp.float32, jnp.bfloat16
N = 128
CAP = 64
GROUP = 16
STEPS = N // GROUP - 1
SLOTS = GROUP * CAP
SENT = CAP + 16
ROWS = 32
C_OBS = 32


def position():
    return lax.axis_index("lat"), lax.axis_index("lon")


def partner(lat, lon, ordinal):
    mixed = lax.rem(ordinal * 37, N)
    z = lax.rem(lat // 2 + lax.rem(mixed // 2, 4), 4)
    core = lax.rem(lat + lax.rem(mixed, 2), 2)
    x = lax.rem(lon // 4 + lax.rem(mixed // 8, 4), 4)
    y = lax.rem(lon + mixed // 32, 4)
    return z * 2 + core, x * 4 + y


NEAR = 22


def greet_near(lat, lon):
    barrier = pltpu.get_barrier_semaphore()
    for d in range(1, 16):
        pl.semaphore_signal(barrier, inc=1, device_id=(lat, lax.rem(lon + d, 16)), device_id_type=MESH)
    for d in range(1, 8):
        pl.semaphore_signal(barrier, inc=1, device_id=(lax.rem(lat + d, 8), lon), device_id_type=MESH)
    return barrier


def pack_values(wide_ref, turned_ref, message_ref):
    for i in range(16):
        pair = jnp.concatenate([wide_ref[:, i, :], wide_ref[:, 16 + i, :]], axis=0)
        turned_ref[:, i, :] = pair.T
    message_ref[:, CAP:, :] = turned_ref[...].astype(BF16)


def pack_codes(blocks_ref, counts_ref, codes_ref):
    slot = lax.broadcasted_iota(jnp.int32, (CAP, N), 0)
    code = jnp.where(slot < counts_ref[...], blocks_ref[...], 4 * ROWS)
    turned = jnp.concatenate([code, code], axis=0).astype(F32).T.astype(jnp.int32)
    codes_ref[:, 0, :] = turned


def spread_group(first, group, got, got_c, perm_ref, lhs_ref, rhs_ref, acc_ref):
    slots = group * CAP
    lane = lax.broadcasted_iota(jnp.int32, (1, N), 1)
    codes = got_c[pl.ds(first, group), 0, :]
    row_parts, value_parts = [], []
    for p in range(group // 2):
        even, odd = codes[2 * p : 2 * p + 1], codes[2 * p + 1 : 2 * p + 2]
        row_parts.append(jnp.where(lane < CAP, even, odd))
        one = got[first + 2 * p, CAP:, :].astype(F32)
        two = got[first + 2 * p + 1, CAP:, :].astype(F32)
        upper = jnp.where(lane < CAP, one, pltpu.roll(two, CAP, 1))
        lower = jnp.where(lane < CAP, pltpu.roll(one, CAP, 1), two)
        value_parts.append(jnp.concatenate([upper, lower], axis=0))
    row_of = jnp.broadcast_to(jnp.concatenate(row_parts, axis=1) // 4, (C_OBS, slots)).astype(F32).astype(BF16)
    values = jnp.concatenate(value_parts, axis=1).astype(BF16)
    zero = jnp.zeros_like(values)
    for r in range(ROWS):
        lhs_ref[r * C_OBS : (r + 1) * C_OBS, :slots] = jnp.where(row_of == jnp.array(r, BF16), values, zero)
    rows = lax.broadcasted_iota(jnp.int32, (ROWS, slots), 0).astype(F32).astype(BF16)
    lhs_ref[ROWS * C_OBS :, :slots] = jnp.where(row_of == rows, jnp.ones_like(values), zero)
    quarter = lax.rem(codes, 4).astype(F32).T
    lane_quarter = (lax.broadcasted_iota(jnp.int32, (CAP, N), 1) // 32).astype(F32)
    for s in range(group):
        keep = jnp.where(quarter[:CAP, s : s + 1] == lane_quarter, 1.0, 0.0).astype(BF16)
        pixels = jnp.dot(got[first + s, :CAP, :], perm_ref[...], preferred_element_type=F32).astype(BF16)
        for phase in range(4):
            rhs_ref[s * CAP : (s + 1) * CAP, phase * N : (phase + 1) * N] = (
                pixels[:, phase * N : (phase + 1) * N] * keep
            )
    acc_ref[...] += jnp.dot(lhs_ref[:, :slots], rhs_ref[:slots, :], preferred_element_type=F32)


def send_to(source, target, sent, came, device):
    return pltpu.make_async_remote_copy(
        src_ref=source, dst_ref=target, send_sem=sent, recv_sem=came, device_id=device, device_id_type=MESH
    )


def sixteenth(ref, p):
    rows = pl.ds(pl.multiple_of(8 * (p // 2), 8), 8)
    return ref.at[rows, pl.ds(pl.multiple_of(512 * lax.rem(p, 2), 512), 512)]


def sum_begin(lat, lon, part_ref, by_lon, sent, came):
    copies = []
    for d in range(1, 16):
        to = lax.rem(lon + d, 16)
        copies.append(send_to(sixteenth(part_ref, to), by_lon.at[d], sent.at[d], came.at[d], (lat, to)))
    for copy in copies:
        copy.start()
    return copies


def sum_end(lat, lon, copies, part_ref, total_ref, by_lon, by_lat, sent, came):
    for copy in copies:
        copy.wait_recv()
    total = sixteenth(part_ref, lon)[...]
    for d in range(1, 16):
        total = total + by_lon[d]
    by_lat[lat] = total
    across = []
    for d in range(1, 8):
        to = lax.rem(lat + d, 8)
        across.append(send_to(by_lat.at[lat], by_lat.at[lat], sent.at[16 + d], came.at[16 + d], (to, lon)))
    for copy in across:
        copy.start()
    for copy in across:
        copy.wait_recv()
    total = by_lat[0]
    for d in range(1, 8):
        total = total + by_lat[d]
    mine = sixteenth(total_ref, lon)
    mine[...] = total
    back = []
    for d in range(1, 16):
        back.append(send_to(mine, mine, sent.at[24 + d], came.at[24 + d], (lat, lax.rem(lon + d, 16))))
    for copy in back:
        copy.start()
    for copy in back:
        copy.wait_recv()
    for copy in copies + across + back:
        copy.wait_send()


CH = 64
STEP_ONE = 5 * C_OBS
STEP_TWO = 3 * CH


def halves(value):
    high = value.astype(BF16)
    return high, (value - high.astype(F32)).astype(BF16)


def dot_nt(a, b):
    return lax.dot_general(a, b, (((1,), (1,)), ((), ())), preferred_element_type=F32)


def dot(a, b):
    return jnp.dot(a, b, preferred_element_type=F32)


def lanes(rows):
    return lax.broadcasted_iota(jnp.int32, (rows, N), 1)


def pack_column(total, place, column):
    return jnp.where(lanes(total.shape[0]) == place, jnp.broadcast_to(column, total.shape), total)


def enter_west(value, column):
    moved = pltpu.roll(value, 1, 1)
    return jnp.where(lanes(value.shape[0]) == 0, jnp.broadcast_to(column, value.shape), moved)


def enter_east(value, column):
    moved = pltpu.roll(value, N - 1, 1)
    return jnp.where(lanes(value.shape[0]) == N - 1, jnp.broadcast_to(column, value.shape), moved)


def arrange_kernels(one_ref, two_ref, wide_one, wide_adj, wide_two, left_one, left_adj, left_two):
    wide_one[...] = jnp.zeros_like(wide_one)
    wide_adj[...] = jnp.zeros_like(wide_adj)
    for a in range(3):
        for tap in range(5):
            row = a * STEP_ONE + tap * C_OBS
            thin = 3 * STEP_ONE + a * 8 + tap
            for half, e in ((0, tap), (1, tap - 2)):
                if 0 <= e < 3:
                    at = slice(half * CH, half * CH + CH)
                    wide_one[row : row + C_OBS, at] = one_ref[a, e, :C_OBS, :]
                    wide_one[thin : thin + 1, at] = one_ref[a, e, C_OBS:, :]
        for e in range(3):
            at = (a * 3 + e) * CH
            wide_two[:, at : at + CH] = two_ref[a, e]
    for lower in range(2):
        for east in range(2):
            for down in range(lower + 1):
                for right in range(east + 1):
                    a = 1 if lower == 0 else 2 - 2 * down
                    e = 1 if east == 0 else 2 - 2 * right
                    row, col = (down * 2 + right) * CH, (lower * 2 + east) * CH
                    wide_adj[row : row + CH, col : col + CH] = two_ref[a, e]
    for wide, left, turn in ((wide_one, left_one, True), (wide_adj, left_adj, True), (wide_two, left_two, False)):
        value = wide[...].T if turn else wide[...]
        high, low = halves(value)
        rows = value.shape[0]
        left[:rows, :] = high
        left[rows:, :] = low


def arrange_cotangent(cot_ref, wide_cot, cot, cot_col):
    wide_cot[...] = cot_ref[...].astype(F32)
    packed = jnp.zeros((CH, N), F32)
    for g in range(8):
        value = wide_cot[:, g, :]
        cot[g] = value
        packed = pack_column(packed, g, value[:, :1])
    cot_col[...] = packed


def back_to_activation(lat, cot, from_south, from_east, from_corner, right, left_adj, grad_act):
    cot[8] = jnp.where(lat < 7, from_south[...], 0.0)
    edge = from_east[...]
    for g in range(9):
        column = edge[:, g : g + 1] if g < 8 else jnp.where(lat < 7, from_corner[:, :1], 0.0)
        right[g] = enter_east(cot[g], column)

    def pair(p, carry):
        stack = [
            jnp.concatenate([cot[g], right[g], cot[g + 1], right[g + 1]], axis=0).astype(BF16)
            for g in (2 * p, 2 * p + 1)
        ]
        both = dot(left_adj[...], jnp.concatenate(stack, axis=1))
        both = both[:256] + both[256:]
        grad_act[2 * p] = both[:, :N]
        grad_act[2 * p + 1] = both[:, N:]
        return carry

    lax.fori_loop(0, 4, pair, 0)


def field_edges(acc_ref, edge_ref):
    packed = jnp.zeros((C_OBS, N), F32)
    for r in range(ROWS):
        packed = pack_column(packed, r, acc_ref[r * C_OBS : (r + 1) * C_OBS, 4 * N - 1 :])
    edge_ref[:C_OBS, :] = packed
    edge_ref[C_OBS:, :] = acc_ref[ROWS * C_OBS :, 3 * N :]


def split_inside(acc_ref, thin, high_ref, low_ref):
    for r in range(ROWS):
        for phase in range(4):
            high, low = halves(acc_ref[r * C_OBS : (r + 1) * C_OBS, phase * N : (phase + 1) * N])
            at = slice((phase + 1) * C_OBS, (phase + 2) * C_OBS)
            high_ref[r + 1, at, :] = high
            low_ref[r + 1, at, :] = low
    thin[...] = jnp.zeros_like(thin)
    for phase in range(4):
        thin[1 : ROWS + 1, phase + 1, :] = acc_ref[ROWS * C_OBS :, phase * N : (phase + 1) * N]


def split_rim(lat, acc_ref, north, north_thin, from_west, from_corner, thin, high_ref, low_ref, thin_high, thin_low):
    for r in range(ROWS):
        moved = enter_west(acc_ref[r * C_OBS : (r + 1) * C_OBS, 3 * N :], from_west[:C_OBS, r : r + 1])
        high, low = halves(moved)
        high_ref[r + 1, :C_OBS, :] = high
        low_ref[r + 1, :C_OBS, :] = low
    inside = lat > 0
    phases = [jnp.where(inside, north[:, phase * N : (phase + 1) * N], 0.0) for phase in range(4)]
    corner = jnp.where(inside, from_corner[:C_OBS, ROWS - 1 : ROWS], 0.0)
    high, low = halves(jnp.concatenate([enter_west(phases[3], corner)] + phases, axis=0))
    high_ref[0] = high
    low_ref[0] = low
    for phase in range(4):
        at = slice(phase * N, (phase + 1) * N)
        thin[0, phase + 1 : phase + 2, :] = jnp.where(inside, north_thin[7:8, at], 0.0)
    thin[1 : ROWS + 1, 0, :] = enter_west(acc_ref[ROWS * C_OBS :, 3 * N :], from_west[C_OBS:, N - 1 :])
    corner = enter_west(north_thin[7:8, 3 * N :], from_corner[2 * C_OBS - 1 :, N - 1 :])
    thin[0, 0:1, :] = jnp.where(inside, corner, 0.0)
    for h in range(ROWS // 2):
        rows = [thin[2 * h], thin[2 * h + 1], thin[2 * h + 2], jnp.zeros((8, N), F32)]
        high, low = halves(jnp.concatenate(rows, axis=0))
        thin_high[h] = high
        thin_low[h] = low


def taps_one(h, field, thin):
    return jnp.concatenate([field[2 * h], field[2 * h + 1], field[2 * h + 2], thin[h]], axis=0)


def taps_two(h, act):
    return jnp.concatenate([act[2 * h], act[2 * h + 1], act[2 * h + 2]], axis=0)


def beside(function, p, *refs):
    return jnp.concatenate([function(2 * p, *refs), function(2 * p + 1, *refs)], axis=1)


def first_layer(field_high, field_low, thin_high, thin_low, left_one, pre, act):
    def pair(p, carry):
        both = dot(left_one[...], beside(taps_one, p, field_high, thin_high))
        out = both[:N] + both[N:] + dot(left_one[:N, :], beside(taps_one, p, field_low, thin_low))
        active = out / (1.0 + jnp.exp(-out))
        for k in range(2):
            pre[2 * p + k] = out[:, k * N : (k + 1) * N]
            act[2 * p + k] = active[:, k * N : (k + 1) * N]
        return carry

    lax.fori_loop(0, ROWS // 4, pair, 0, unroll=4)


def first_gradient(field_high, field_low, thin_high, thin_low, pre, grad_act):
    def row(h, g, lower):
        value = pre[h]
        s = 1.0 / (1.0 + jnp.exp(-value))
        return grad_act[g, lower * N : (lower + 1) * N, :] * (s * (1.0 + value * (1.0 - s)))

    def pair(p, total):
        grad = jnp.concatenate([row(2 * p, p, 0), row(2 * p + 1, p, 1)], axis=1)
        high, low = halves(grad)
        field = beside(taps_one, p, field_high, thin_high)
        both = dot_nt(jnp.concatenate([high, low], axis=0), field)
        return total + (both[:N] + both[N:]) + dot_nt(high, beside(taps_one, p, field_low, thin_low))

    return lax.fori_loop(0, ROWS // 4, pair, jnp.zeros((N, 4 * N), F32), unroll=4)


def activation_edges(act, edge_ref):
    packed = jnp.zeros((CH, N), F32)
    for y in range(ROWS // 2):
        packed = pack_column(packed, y, act[y, CH:, N - 1 :])
    edge_ref[...] = packed


def split_activation_inside(act, high_ref, low_ref):
    for y in range(ROWS // 2):
        high, low = halves(act[y])
        high_ref[y + 1, CH:, :] = high
        low_ref[y + 1, CH:, :] = low


def split_activation_rim(lat, act, north, from_west, from_corner, high_ref, low_ref):
    for y in range(ROWS // 2):
        high, low = halves(enter_west(act[y, CH:, :], from_west[:, y : y + 1]))
        high_ref[y + 1, :CH, :] = high
        low_ref[y + 1, :CH, :] = low
    last = ROWS // 2 - 1
    value = jnp.where(lat > 0, north[...], 0.0)
    column = jnp.where(lat > 0, from_corner[:, last : last + 1], 0.0)
    high, low = halves(jnp.concatenate([enter_west(value[CH:], column), value], axis=0))
    high_ref[0] = high
    low_ref[0] = low


def second_gradient(act_high, act_low, cot):
    total = jnp.zeros((CH, 9 * CH), F32)
    for p in range(4):
        grad = jnp.concatenate([cot[2 * p], cot[2 * p + 1]], axis=1).astype(BF16)
        total = total + (dot_nt(grad, beside(taps_two, p, act_high)) + dot_nt(grad, beside(taps_two, p, act_low)))
    return total


def second_layer(act_high, act_low, left_two, wide_features):
    for p in range(4):
        both = dot(left_two[...], beside(taps_two, p, act_high))
        out = both[:CH] + both[CH:] + dot(left_two[:CH, :], beside(taps_two, p, act_low))
        for k in range(2):
            wide_features[:, 2 * p + k, :] = out[:, k * N : (k + 1) * N]


def pack_first_gradient(one, part_ref):
    lane = lax.broadcasted_iota(jnp.int32, (CH, 4 * N), 1)
    upper, lower = one[:CH], one[CH:]
    moved = jnp.where(lane < 3 * STEP_ONE, pltpu.roll(lower, 4 * N - 2 * C_OBS, 1), pltpu.roll(lower, 4 * N - 2, 1))
    both = upper + moved
    tight = jnp.where(
        lane < 96, both,
        jnp.where(
            lane < 192, pltpu.roll(both, 4 * N - 64, 1),
            jnp.where(lane < 288, pltpu.roll(both, 4 * N - 128, 1), pltpu.roll(both, 4 * N - 192, 1)),
        ),
    )
    shifted = pltpu.roll(tight, CH, 1)
    part_ref[:, 4 * N :] = shifted


def unpack_gradients(total_ref, one_ref, two_ref):
    for i in range(9):
        two_ref[i] = total_ref[:, i * CH : (i + 1) * CH]
    turned = total_ref[:, 4 * N : 7 * N].T
    for i in range(9):
        one_ref[i, :C_OBS, :] = turned[CH + i * C_OBS : CH + (i + 1) * C_OBS]
        thin = CH + 9 * C_OBS + (i // 3) * 8 + i % 3
        one_ref[i, C_OBS:, :] = turned[thin : thin + 1]


def arrange_picker(picker_ref):
    lane = lax.broadcasted_iota(jnp.int32, (N, 4 * N), 1)
    pixel = lax.broadcasted_iota(jnp.int32, (N, 4 * N), 0)
    picker_ref[...] = jnp.where(pixel == 4 * lax.rem(lane, 32) + lane // N, 1.0, 0.0).astype(BF16)


class Named:
    def __init__(self, names, refs):
        self.__dict__.update(zip(names, refs))


SCRATCH = {
    "wide": pltpu.VMEM((CAP, C_OBS, N), F32),
    "turned": pltpu.VMEM((N, 16, N), F32),
    "codes": pltpu.VMEM((N, 1, N), jnp.int32),
    "got_codes": pltpu.VMEM((N, 1, N), jnp.int32),
    "message": pltpu.VMEM((N, SENT, N), BF16),
    "got": pltpu.VMEM((N, SENT, N), BF16),
    "lhs": pltpu.VMEM((ROWS * C_OBS + ROWS, SLOTS), BF16),
    "rhs": pltpu.VMEM((SLOTS, 4 * N), BF16),
    "acc": pltpu.VMEM((ROWS * C_OBS + ROWS, 4 * N), F32),
    "wide_one": pltpu.VMEM((4 * N, N), F32),
    "wide_adj": pltpu.VMEM((256, 256), F32),
    "wide_two": pltpu.VMEM((CH, 9 * CH), F32),
    "left_one": pltpu.VMEM((256, 4 * N), BF16),
    "left_adj": pltpu.VMEM((512, 256), BF16),
    "left_two": pltpu.VMEM((N, 9 * CH), BF16),
    "wide_cot": pltpu.VMEM((CH, 8, N), F32),
    "cot": pltpu.VMEM((9, CH, N), F32),
    "cot_right": pltpu.VMEM((9, CH, N), F32),
    "cot_col": pltpu.VMEM((CH, N), F32),
    "cot_south": pltpu.VMEM((CH, N), F32),
    "cot_east": pltpu.VMEM((CH, N), F32),
    "cot_corner": pltpu.VMEM((CH, N), F32),
    "grad_act": pltpu.VMEM((8, 256, N), F32),
    "edge": pltpu.VMEM((2 * C_OBS, N), F32),
    "edge_west": pltpu.VMEM((2 * C_OBS, N), F32),
    "edge_corner": pltpu.VMEM((2 * C_OBS, N), F32),
    "north": pltpu.VMEM((C_OBS, 4 * N), F32),
    "north_thin": pltpu.VMEM((8, 4 * N), F32),
    "thin": pltpu.VMEM((ROWS + 1, 8, N), F32),
    "field_high": pltpu.VMEM((ROWS + 1, STEP_ONE, N), BF16),
    "field_low": pltpu.VMEM((ROWS + 1, STEP_ONE, N), BF16),
    "thin_high": pltpu.VMEM((ROWS // 2, 32, N), BF16),
    "thin_low": pltpu.VMEM((ROWS // 2, 32, N), BF16),
    "pre": pltpu.VMEM((ROWS // 2, N, N), F32),
    "act": pltpu.VMEM((ROWS // 2, N, N), F32),
    "act_edge": pltpu.VMEM((CH, N), F32),
    "act_west": pltpu.VMEM((CH, N), F32),
    "act_corner": pltpu.VMEM((CH, N), F32),
    "act_north": pltpu.VMEM((N, N), F32),
    "act_high": pltpu.VMEM((ROWS // 2 + 1, STEP_TWO, N), BF16),
    "act_low": pltpu.VMEM((ROWS // 2 + 1, STEP_TWO, N), BF16),
    "grad_one": pltpu.VMEM((9, C_OBS + 1, CH), F32),
    "grad_two": pltpu.VMEM((9, CH, CH), F32),
    "features": pltpu.VMEM((CH, 8, N), BF16),
    "wide_features": pltpu.VMEM((CH, 8, N), F32),
    "part": pltpu.VMEM((CH, 8 * N), F32),
    "total": pltpu.VMEM((CH, 8 * N), F32),
    "by_lon": pltpu.VMEM((16, 8, 4 * N), F32),
    "by_lat": pltpu.VMEM((8, 8, 4 * N), F32),
    "sent": pltpu.SemaphoreType.DMA((2,)),
    "came": pltpu.SemaphoreType.DMA((2, STEPS + 2)),
    "values": pltpu.VMEM((CAP, C_OBS, N), BF16),
    "blocks": pltpu.VMEM((CAP, N), jnp.int32),
    "counts": pltpu.VMEM((1, N), jnp.int32),
    "cot_in": pltpu.VMEM((CH, 8, N), BF16),
    "one": pltpu.VMEM((3, 3, C_OBS + 1, CH), F32),
    "two": pltpu.VMEM((3, 3, CH, CH), F32),
    "picker": pltpu.VMEM((N, 4 * N), BF16),
    "fetch": pltpu.SemaphoreType.DMA((7,)),
    "met": pltpu.SemaphoreType.REGULAR,
    "own": pltpu.SemaphoreType.DMA((2,)),
    "result": pltpu.SemaphoreType.DMA((3,)),
    "halo_sent": pltpu.SemaphoreType.DMA((10,)),
    "halo_came": pltpu.SemaphoreType.DMA((10,)),
    "sum_sent": pltpu.SemaphoreType.DMA((40,)),
    "sum_came": pltpu.SemaphoreType.DMA((40,)),
}


def whole_kernel(
    values_ref, w_ref, blocks_ref, counts_ref, one_ref, two_ref, cot_ref,
    features_ref, grad_one_ref, grad_two_ref, *scratch,
):
    m = Named(SCRATCH, scratch)
    lat, lon = position()
    me = lat * 16 + lon
    barrier = greet_near(lat, lon)
    fetched = [
        pltpu.make_async_copy(source, target, m.fetch.at[k])
        for k, (source, target) in enumerate((
            (values_ref, m.values), (blocks_ref, m.blocks), (counts_ref, m.counts),
            (w_ref, m.message.at[:, pl.ds(0, CAP)]),
            (cot_ref, m.cot_in), (one_ref, m.one), (two_ref, m.two),
        ))
    ]
    for copy in fetched:
        copy.start()
    arrange_picker(m.picker)

    north, south = lax.rem(lat + 7, 8), lax.rem(lat + 1, 8)
    west, east = lax.rem(lon + 15, 16), lax.rem(lon + 1, 16)

    def halo(k, source, target, device):
        return send_to(source, target, m.halo_sent.at[k], m.halo_came.at[k], device)

    pl.semaphore_wait(barrier, NEAR)
    for d in range(1, 16):
        pl.semaphore_signal(m.met, inc=1, device_id=(lat, lax.rem(lon + d, 16)), device_id_type=MESH)
    fetched[0].wait()
    m.wide[...] = m.values[...].astype(F32)
    pack_values(m.wide, m.turned, m.message)
    fetched[1].wait()
    fetched[2].wait()
    pack_codes(m.blocks, m.counts, m.codes)
    fetched[3].wait()
    streams = ((m.message, m.got), (m.codes, m.got_codes))
    mine = [
        pltpu.make_async_copy(source.at[me], target.at[0], m.own.at[k]) for k, (source, target) in enumerate(streams)
    ]
    for copy in mine:
        copy.start()
    def send(ordinal, carry):
        to_lat, to_lon = partner(lat, lon, ordinal)
        step = jnp.where(ordinal < STEPS * GROUP, ordinal // GROUP, ordinal // (GROUP // 2) - STEPS)
        to = to_lat * 16 + to_lon
        for k, (source, target) in enumerate(streams):
            send_to(
                source.at[to], target.at[ordinal], m.sent.at[k], m.came.at[k, step], (to_lat, to_lon)
            ).start()
        return carry

    fetched[4].wait()
    arrange_cotangent(m.cot_in, m.wide_cot, m.cot, m.cot_col)
    cot_halo = [
        halo(0, m.cot_col, m.cot_east, (lat, west)),
        halo(1, m.cot.at[0], m.cot_south, (north, lon)),
        halo(2, m.cot_col, m.cot_corner, (north, west)),
    ]
    cot_halo[0].start()
    cot_halo[1].start()
    pl.semaphore_wait(m.met, 15)
    cot_halo[2].start()
    lax.fori_loop(1, N, send, 0)

    fetched[5].wait()
    fetched[6].wait()
    arrange_kernels(m.one, m.two, m.wide_one, m.wide_adj, m.wide_two, m.left_one, m.left_adj, m.left_two)
    m.acc[...] = jnp.zeros_like(m.acc)
    for copy in cot_halo:
        copy.wait()
    back_to_activation(
        lat, m.cot, m.cot_south, m.cot_east, m.cot_corner, m.cot_right, m.left_adj, m.grad_act
    )
    for copy in mine:
        copy.wait()

    def arrive(first, count, step):
        for k, (_, target) in enumerate(streams):
            part = target.at[pl.ds(first, count)]
            pltpu.make_async_copy(part, part, m.came.at[k, step]).wait()

    def spread(first, group):
        spread_group(first, group, m.got, m.got_codes, m.picker, m.lhs, m.rhs, m.acc)

    def work(step, carry):
        @pl.when(step == 0)
        def _():
            arrive(1, GROUP - 1, 0)

        @pl.when(step > 0)
        def _():
            arrive(step * GROUP, GROUP, step)

        spread(step * GROUP, GROUP)
        return carry

    lax.fori_loop(0, STEPS, work, 0)

    def work_half(step, carry):
        first = STEPS * GROUP + step * (GROUP // 2)
        arrive(first, GROUP // 2, STEPS + step)
        spread(first, GROUP // 2)
        return carry

    lax.fori_loop(0, 2, work_half, 0)

    last = ROWS * C_OBS
    rows_halo = [
        halo(3, m.acc.at[pl.ds(last - C_OBS, C_OBS)], m.north, (south, lon)),
        halo(4, m.acc.at[pl.ds(last + ROWS - 8, 8)], m.north_thin, (south, lon)),
    ]
    edge_halo = [
        halo(5, m.edge, m.edge_west, (lat, east)),
        halo(6, m.edge, m.edge_corner, (south, east)),
    ]
    for copy in rows_halo:
        copy.start()
    field_edges(m.acc, m.edge)
    for copy in edge_halo:
        copy.start()
    split_inside(m.acc, m.thin, m.field_high, m.field_low)
    for copy in edge_halo + rows_halo:
        copy.wait()
    split_rim(
        lat, m.acc, m.north, m.north_thin, m.edge_west, m.edge_corner, m.thin,
        m.field_high, m.field_low, m.thin_high, m.thin_low,
    )
    field = (m.field_high, m.field_low, m.thin_high, m.thin_low)
    first_layer(*field, m.left_one, m.pre, m.act)
    act_halo = [
        halo(7, m.act.at[ROWS // 2 - 1], m.act_north, (south, lon)),
        halo(8, m.act_edge, m.act_west, (lat, east)),
        halo(9, m.act_edge, m.act_corner, (south, east)),
    ]
    act_halo[0].start()
    activation_edges(m.act, m.act_edge)
    act_halo[1].start()
    act_halo[2].start()
    grad_one = first_gradient(*field, m.pre, m.grad_act)
    pack_first_gradient(grad_one, m.part)
    split_activation_inside(m.act, m.act_high, m.act_low)
    for copy in act_halo:
        copy.wait()
    split_activation_rim(lat, m.act, m.act_north, m.act_west, m.act_corner, m.act_high, m.act_low)
    m.part[:, : 9 * CH] = second_gradient(m.act_high, m.act_low, m.cot)
    first_leg = sum_begin(lat, lon, m.part, m.by_lon, m.sum_sent, m.sum_came)
    second_layer(m.act_high, m.act_low, m.left_two, m.wide_features)
    m.features[...] = m.wide_features[...].astype(BF16)
    results = [
        pltpu.make_async_copy(m.features, features_ref, m.result.at[0]),
        pltpu.make_async_copy(m.grad_one, grad_one_ref, m.result.at[1]),
        pltpu.make_async_copy(m.grad_two, grad_two_ref, m.result.at[2]),
    ]
    results[0].start()
    sum_end(lat, lon, first_leg, m.part, m.total, m.by_lon, m.by_lat, m.sum_sent, m.sum_came)
    unpack_gradients(m.total, m.grad_one, m.grad_two)
    results[1].start()
    results[2].start()
    for k, (_, target) in enumerate(streams):
        everything = target.at[pl.ds(0, N - 1)]
        pltpu.make_async_copy(everything, everything, m.sent.at[k]).wait()
    for copy in results:
        copy.wait()


def hand_on_kernel(*refs):
    for k in range(3):
        refs[3 + k][...] = refs[k][...]


def on_device(
    obs_values, kernel_weights, pixel_blocks, obs_counts, kernel_one, kernel_two, cotangent
):
    vmem, anywhere = pl.BlockSpec(memory_space=pltpu.VMEM), pl.BlockSpec(memory_space=pl.ANY)
    outputs = (
        jax.ShapeDtypeStruct((CH, 8, N), BF16),
        jax.ShapeDtypeStruct((9, C_OBS + 1, CH), F32),
        jax.ShapeDtypeStruct((9, CH, CH), F32),
    )
    results = pl.pallas_call(
        whole_kernel,
        out_shape=outputs,
        in_specs=[anywhere] * 7,
        out_specs=(anywhere,) * 3,
        scratch_shapes=list(SCRATCH.values()),
        compiler_params=pltpu.CompilerParams(collective_id=0, has_side_effects=True, vmem_limit_bytes=56 << 20),
    )(
        obs_values[0].transpose(1, 2, 0),
        kernel_weights[0],
        pixel_blocks[0].T,
        obs_counts,
        kernel_one.transpose(0, 1, 3, 2),
        kernel_two,
        cotangent,
    )
    features, grad_one, grad_two = pl.pallas_call(
        hand_on_kernel,
        out_shape=outputs,
        in_specs=[vmem] * 3,
        out_specs=(vmem,) * 3,
        scratch_shapes=[pltpu.SemaphoreType.DMA((3,))],
    )(*results)
    grad_one = grad_one.reshape(3, 3, C_OBS + 1, CH).transpose(0, 1, 3, 2)
    return features, grad_one, grad_two.reshape(3, 3, CH, CH)


def solution(mesh):
    placed = (
        P(("lat", "lon"), None, None, None),
        P(("lat", "lon"), None, None, None),
        P(("lat", "lon"), None, None),
        P(("lat", "lon"), None),
        P(),
        P(),
        P(None, "lat", "lon"),
    )
    return jax.shard_map(
        on_device,
        mesh=mesh,
        in_specs=placed,
        out_specs=(P(None, "lat", "lon"), P(), P()),
        check_vma=False,
    )
```

```python
import jax
import jax.numpy as jnp
from jax import lax
from jax.experimental import pallas as pl
from jax.experimental.pallas import tpu as pltpu
from jax.sharding import PartitionSpec as P

MESH = pl.DeviceIdType.MESH
F32, BF16 = jnp.float32, jnp.bfloat16
N = 128
CAP = 64
GROUP = 16
STEPS = N // GROUP - 1
SLOTS = GROUP * CAP
SENT = CAP + 16
ROWS = 32
C_OBS = 32


def position():
    return lax.axis_index("lat"), lax.axis_index("lon")


def partner(lat, lon, ordinal):
    mixed = lax.rem(ordinal * 37, N)
    z = lax.rem(lat // 2 + lax.rem(mixed // 2, 4), 4)
    core = lax.rem(lat + lax.rem(mixed, 2), 2)
    x = lax.rem(lon // 4 + lax.rem(mixed // 8, 4), 4)
    y = lax.rem(lon + mixed // 32, 4)
    return z * 2 + core, x * 4 + y


NEAR = 22


def greet_near(lat, lon):
    barrier = pltpu.get_barrier_semaphore()
    for d in range(1, 16):
        pl.semaphore_signal(barrier, inc=1, device_id=(lat, lax.rem(lon + d, 16)), device_id_type=MESH)
    for d in range(1, 8):
        pl.semaphore_signal(barrier, inc=1, device_id=(lax.rem(lat + d, 8), lon), device_id_type=MESH)
    return barrier


def pack_values(wide_ref, turned_ref, message_ref):
    for i in range(16):
        pair = jnp.concatenate([wide_ref[:, i, :], wide_ref[:, 16 + i, :]], axis=0)
        turned_ref[:, i, :] = pair.T
    message_ref[:, CAP:, :] = turned_ref[...].astype(BF16)


def pack_codes(blocks_ref, counts_ref, codes_ref):
    slot = lax.broadcasted_iota(jnp.int32, (CAP, N), 0)
    code = jnp.where(slot < counts_ref[...], blocks_ref[...], 4 * ROWS)
    turned = jnp.concatenate([code, code], axis=0).astype(F32).T.astype(jnp.int32)
    codes_ref[:, 0, :] = turned


def spread_group(first, group, got, got_c, perm_ref, lhs_ref, rhs_ref, acc_ref):
    slots = group * CAP
    lane = lax.broadcasted_iota(jnp.int32, (1, N), 1)
    codes = got_c[pl.ds(first, group), 0, :]
    row_parts, value_parts = [], []
    for p in range(group // 2):
        even, odd = codes[2 * p : 2 * p + 1], codes[2 * p + 1 : 2 * p + 2]
        row_parts.append(jnp.where(lane < CAP, even, odd))
        one = got[first + 2 * p, CAP:, :].astype(F32)
        two = got[first + 2 * p + 1, CAP:, :].astype(F32)
        upper = jnp.where(lane < CAP, one, pltpu.roll(two, CAP, 1))
        lower = jnp.where(lane < CAP, pltpu.roll(one, CAP, 1), two)
        value_parts.append(jnp.concatenate([upper, lower], axis=0))
    row_of = jnp.broadcast_to(jnp.concatenate(row_parts, axis=1) // 4, (C_OBS, slots)).astype(F32).astype(BF16)
    values = jnp.concatenate(value_parts, axis=1).astype(BF16)
    zero = jnp.zeros_like(values)
    for r in range(ROWS):
        lhs_ref[r * C_OBS : (r + 1) * C_OBS, :slots] = jnp.where(row_of == jnp.array(r, BF16), values, zero)
    rows = lax.broadcasted_iota(jnp.int32, (ROWS, slots), 0).astype(F32).astype(BF16)
    lhs_ref[ROWS * C_OBS :, :slots] = jnp.where(row_of == rows, jnp.ones_like(values), zero)
    quarter = lax.rem(codes, 4).astype(F32).T
    lane_quarter = (lax.broadcasted_iota(jnp.int32, (CAP, N), 1) // 32).astype(F32)
    for s in range(group):
        keep = jnp.where(quarter[:CAP, s : s + 1] == lane_quarter, 1.0, 0.0).astype(BF16)
        pixels = jnp.dot(got[first + s, :CAP, :], perm_ref[...], preferred_element_type=F32).astype(BF16)
        for phase in range(4):
            rhs_ref[s * CAP : (s + 1) * CAP, phase * N : (phase + 1) * N] = (
                pixels[:, phase * N : (phase + 1) * N] * keep
            )
    acc_ref[...] += jnp.dot(lhs_ref[:, :slots], rhs_ref[:slots, :], preferred_element_type=F32)


def send_to(source, target, sent, came, device):
    return pltpu.make_async_remote_copy(
        src_ref=source, dst_ref=target, send_sem=sent, recv_sem=came, device_id=device, device_id_type=MESH
    )


AROUND = sorted(
    ((dx, dy) for dx in range(4) for dy in range(4) if dx + dy > 0),
    key=lambda at: -min(at[0], 4 - at[0]) - min(at[1], 4 - at[1]),
)


def around(lon, at):
    return lax.rem(lon // 4 + at[0], 4) * 4 + lax.rem(lon + at[1], 4)


def sixteenth(ref, p):
    rows = pl.ds(pl.multiple_of(8 * (p // 2), 8), 8)
    return ref.at[rows, pl.ds(pl.multiple_of(512 * lax.rem(p, 2), 512), 512)]


def sum_begin(lat, lon, part_ref, by_lon, sent, came):
    copies = []
    for d, at in enumerate(AROUND, 1):
        to = around(lon, at)
        copies.append(send_to(sixteenth(part_ref, to), by_lon.at[d], sent.at[d], came.at[d], (lat, to)))
    for copy in copies:
        copy.start()
    return copies


def sum_end(lat, lon, copies, part_ref, total_ref, by_lon, by_lat, sent, came):
    for copy in copies:
        copy.wait_recv()
    total = sixteenth(part_ref, lon)[...]
    for d in range(1, 16):
        total = total + by_lon[d]
    by_lat[lat] = total
    across = []
    for d in range(1, 8):
        to = lax.rem(lat + d, 8)
        across.append(send_to(by_lat.at[lat], by_lat.at[lat], sent.at[16 + d], came.at[16 + d], (to, lon)))
    for copy in across:
        copy.start()
    for copy in across:
        copy.wait_recv()
    total = by_lat[0]
    for d in range(1, 8):
        total = total + by_lat[d]
    mine = sixteenth(total_ref, lon)
    mine[...] = total
    back = []
    for d, at in enumerate(AROUND, 1):
        back.append(send_to(mine, mine, sent.at[24 + d], came.at[24 + d], (lat, around(lon, at))))
    for copy in back:
        copy.start()
    for copy in back:
        copy.wait_recv()
    for copy in copies + across + back:
        copy.wait_send()


CH = 64
STEP_ONE = 5 * C_OBS
STEP_TWO = 3 * CH


def halves(value):
    high = value.astype(BF16)
    return high, (value - high.astype(F32)).astype(BF16)


def dot_nt(a, b):
    return lax.dot_general(a, b, (((1,), (1,)), ((), ())), preferred_element_type=F32)


def dot(a, b):
    return jnp.dot(a, b, preferred_element_type=F32)


def lanes(rows):
    return lax.broadcasted_iota(jnp.int32, (rows, N), 1)


def pack_column(total, place, column):
    return jnp.where(lanes(total.shape[0]) == place, jnp.broadcast_to(column, total.shape), total)


def enter_west(value, column):
    moved = pltpu.roll(value, 1, 1)
    return jnp.where(lanes(value.shape[0]) == 0, jnp.broadcast_to(column, value.shape), moved)


def enter_east(value, column):
    moved = pltpu.roll(value, N - 1, 1)
    return jnp.where(lanes(value.shape[0]) == N - 1, jnp.broadcast_to(column, value.shape), moved)


def arrange_kernels(one_ref, two_ref, wide_one, wide_adj, wide_two, left_one, left_adj, left_two):
    wide_one[...] = jnp.zeros_like(wide_one)
    wide_adj[...] = jnp.zeros_like(wide_adj)
    for a in range(3):
        for tap in range(5):
            row = a * STEP_ONE + tap * C_OBS
            thin = 3 * STEP_ONE + a * 8 + tap
            for half, e in ((0, tap), (1, tap - 2)):
                if 0 <= e < 3:
                    at = slice(half * CH, half * CH + CH)
                    wide_one[row : row + C_OBS, at] = one_ref[a, e, :C_OBS, :]
                    wide_one[thin : thin + 1, at] = one_ref[a, e, C_OBS:, :]
        for e in range(3):
            at = (a * 3 + e) * CH
            wide_two[:, at : at + CH] = two_ref[a, e]
    for lower in range(2):
        for east in range(2):
            for down in range(lower + 1):
                for right in range(east + 1):
                    a = 1 if lower == 0 else 2 - 2 * down
                    e = 1 if east == 0 else 2 - 2 * right
                    row, col = (down * 2 + right) * CH, (lower * 2 + east) * CH
                    wide_adj[row : row + CH, col : col + CH] = two_ref[a, e]
    for wide, left, turn in ((wide_one, left_one, True), (wide_adj, left_adj, True), (wide_two, left_two, False)):
        value = wide[...].T if turn else wide[...]
        high, low = halves(value)
        rows = value.shape[0]
        left[:rows, :] = high
        left[rows:, :] = low


def arrange_cotangent(cot_ref, wide_cot, cot, cot_col):
    wide_cot[...] = cot_ref[...].astype(F32)
    packed = jnp.zeros((CH, N), F32)
    for g in range(8):
        value = wide_cot[:, g, :]
        cot[g] = value
        packed = pack_column(packed, g, value[:, :1])
    cot_col[...] = packed


def back_to_activation(lat, cot, from_south, from_east, from_corner, right, left_adj, grad_act):
    cot[8] = jnp.where(lat < 7, from_south[...], 0.0)
    edge = from_east[...]
    for g in range(9):
        column = edge[:, g : g + 1] if g < 8 else jnp.where(lat < 7, from_corner[:, :1], 0.0)
        right[g] = enter_east(cot[g], column)

    def pair(p, carry):
        stack = [
            jnp.concatenate([cot[g], right[g], cot[g + 1], right[g + 1]], axis=0).astype(BF16)
            for g in (2 * p, 2 * p + 1)
        ]
        both = dot(left_adj[...], jnp.concatenate(stack, axis=1))
        both = both[:256] + both[256:]
        grad_act[2 * p] = both[:, :N]
        grad_act[2 * p + 1] = both[:, N:]
        return carry

    lax.fori_loop(0, 4, pair, 0)


def field_edges(acc_ref, edge_ref):
    packed = jnp.zeros((C_OBS, N), F32)
    for r in range(ROWS):
        packed = pack_column(packed, r, acc_ref[r * C_OBS : (r + 1) * C_OBS, 4 * N - 1 :])
    edge_ref[:C_OBS, :] = packed
    edge_ref[C_OBS:, :] = acc_ref[ROWS * C_OBS :, 3 * N :]


def split_inside(acc_ref, thin, high_ref, low_ref):
    for r in range(ROWS):
        for phase in range(4):
            high, low = halves(acc_ref[r * C_OBS : (r + 1) * C_OBS, phase * N : (phase + 1) * N])
            at = slice((phase + 1) * C_OBS, (phase + 2) * C_OBS)
            high_ref[r + 1, at, :] = high
            low_ref[r + 1, at, :] = low
    thin[...] = jnp.zeros_like(thin)
    for phase in range(4):
        thin[1 : ROWS + 1, phase + 1, :] = acc_ref[ROWS * C_OBS :, phase * N : (phase + 1) * N]


def split_rim(lat, acc_ref, north, north_thin, from_west, from_corner, thin, high_ref, low_ref, thin_high, thin_low):
    for r in range(ROWS):
        moved = enter_west(acc_ref[r * C_OBS : (r + 1) * C_OBS, 3 * N :], from_west[:C_OBS, r : r + 1])
        high, low = halves(moved)
        high_ref[r + 1, :C_OBS, :] = high
        low_ref[r + 1, :C_OBS, :] = low
    inside = lat > 0
    phases = [jnp.where(inside, north[:, phase * N : (phase + 1) * N], 0.0) for phase in range(4)]
    corner = jnp.where(inside, from_corner[:C_OBS, ROWS - 1 : ROWS], 0.0)
    high, low = halves(jnp.concatenate([enter_west(phases[3], corner)] + phases, axis=0))
    high_ref[0] = high
    low_ref[0] = low
    for phase in range(4):
        at = slice(phase * N, (phase + 1) * N)
        thin[0, phase + 1 : phase + 2, :] = jnp.where(inside, north_thin[7:8, at], 0.0)
    thin[1 : ROWS + 1, 0, :] = enter_west(acc_ref[ROWS * C_OBS :, 3 * N :], from_west[C_OBS:, N - 1 :])
    corner = enter_west(north_thin[7:8, 3 * N :], from_corner[2 * C_OBS - 1 :, N - 1 :])
    thin[0, 0:1, :] = jnp.where(inside, corner, 0.0)
    for h in range(ROWS // 2):
        rows = [thin[2 * h], thin[2 * h + 1], thin[2 * h + 2], jnp.zeros((8, N), F32)]
        high, low = halves(jnp.concatenate(rows, axis=0))
        thin_high[h] = high
        thin_low[h] = low


def taps_one(h, field, thin):
    return jnp.concatenate([field[2 * h], field[2 * h + 1], field[2 * h + 2], thin[h]], axis=0)


def taps_two(h, act):
    return jnp.concatenate([act[2 * h], act[2 * h + 1], act[2 * h + 2]], axis=0)


def beside(function, p, *refs):
    return jnp.concatenate([function(2 * p, *refs), function(2 * p + 1, *refs)], axis=1)


def first_layer(field_high, field_low, thin_high, thin_low, left_one, pre, act):
    def pair(p, carry):
        both = dot(left_one[...], beside(taps_one, p, field_high, thin_high))
        out = both[:N] + both[N:] + dot(left_one[:N, :], beside(taps_one, p, field_low, thin_low))
        active = out / (1.0 + jnp.exp(-out))
        for k in range(2):
            pre[2 * p + k] = out[:, k * N : (k + 1) * N]
            act[2 * p + k] = active[:, k * N : (k + 1) * N]
        return carry

    lax.fori_loop(0, ROWS // 4, pair, 0, unroll=4)


def first_gradient(field_high, field_low, thin_high, thin_low, pre, grad_act):
    def row(h, g, lower):
        value = pre[h]
        s = 1.0 / (1.0 + jnp.exp(-value))
        return grad_act[g, lower * N : (lower + 1) * N, :] * (s * (1.0 + value * (1.0 - s)))

    def pair(p, total):
        grad = jnp.concatenate([row(2 * p, p, 0), row(2 * p + 1, p, 1)], axis=1)
        high, low = halves(grad)
        field = beside(taps_one, p, field_high, thin_high)
        both = dot_nt(jnp.concatenate([high, low], axis=0), field)
        return total + (both[:N] + both[N:]) + dot_nt(high, beside(taps_one, p, field_low, thin_low))

    return lax.fori_loop(0, ROWS // 4, pair, jnp.zeros((N, 4 * N), F32), unroll=4)


def activation_edges(act, edge_ref):
    packed = jnp.zeros((CH, N), F32)
    for y in range(ROWS // 2):
        packed = pack_column(packed, y, act[y, CH:, N - 1 :])
    edge_ref[...] = packed


def split_activation_inside(act, high_ref, low_ref):
    for y in range(ROWS // 2):
        high, low = halves(act[y])
        high_ref[y + 1, CH:, :] = high
        low_ref[y + 1, CH:, :] = low


def split_activation_rim(lat, act, north, from_west, from_corner, high_ref, low_ref):
    for y in range(ROWS // 2):
        high, low = halves(enter_west(act[y, CH:, :], from_west[:, y : y + 1]))
        high_ref[y + 1, :CH, :] = high
        low_ref[y + 1, :CH, :] = low
    last = ROWS // 2 - 1
    value = jnp.where(lat > 0, north[...], 0.0)
    column = jnp.where(lat > 0, from_corner[:, last : last + 1], 0.0)
    high, low = halves(jnp.concatenate([enter_west(value[CH:], column), value], axis=0))
    high_ref[0] = high
    low_ref[0] = low


def second_gradient(act_high, act_low, cot):
    total = jnp.zeros((CH, 9 * CH), F32)
    for p in range(4):
        grad = jnp.concatenate([cot[2 * p], cot[2 * p + 1]], axis=1).astype(BF16)
        total = total + (dot_nt(grad, beside(taps_two, p, act_high)) + dot_nt(grad, beside(taps_two, p, act_low)))
    return total


def second_layer(act_high, act_low, left_two, wide_features):
    for p in range(4):
        both = dot(left_two[...], beside(taps_two, p, act_high))
        out = both[:CH] + both[CH:] + dot(left_two[:CH, :], beside(taps_two, p, act_low))
        for k in range(2):
            wide_features[:, 2 * p + k, :] = out[:, k * N : (k + 1) * N]


def pack_first_gradient(one, part_ref):
    lane = lax.broadcasted_iota(jnp.int32, (CH, 4 * N), 1)
    upper, lower = one[:CH], one[CH:]
    moved = jnp.where(lane < 3 * STEP_ONE, pltpu.roll(lower, 4 * N - 2 * C_OBS, 1), pltpu.roll(lower, 4 * N - 2, 1))
    both = upper + moved
    tight = jnp.where(
        lane < 96, both,
        jnp.where(
            lane < 192, pltpu.roll(both, 4 * N - 64, 1),
            jnp.where(lane < 288, pltpu.roll(both, 4 * N - 128, 1), pltpu.roll(both, 4 * N - 192, 1)),
        ),
    )
    shifted = pltpu.roll(tight, CH, 1)
    part_ref[:, 4 * N :] = shifted


def unpack_gradients(total_ref, one_ref, two_ref):
    for i in range(9):
        two_ref[i] = total_ref[:, i * CH : (i + 1) * CH]
    turned = total_ref[:, 4 * N : 7 * N].T
    for i in range(9):
        one_ref[i, :C_OBS, :] = turned[CH + i * C_OBS : CH + (i + 1) * C_OBS]
        thin = CH + 9 * C_OBS + (i // 3) * 8 + i % 3
        one_ref[i, C_OBS:, :] = turned[thin : thin + 1]


def arrange_picker(picker_ref):
    lane = lax.broadcasted_iota(jnp.int32, (N, 4 * N), 1)
    pixel = lax.broadcasted_iota(jnp.int32, (N, 4 * N), 0)
    picker_ref[...] = jnp.where(pixel == 4 * lax.rem(lane, 32) + lane // N, 1.0, 0.0).astype(BF16)


class Named:
    def __init__(self, names, refs):
        self.__dict__.update(zip(names, refs))


SCRATCH = {
    "wide": pltpu.VMEM((CAP, C_OBS, N), F32),
    "turned": pltpu.VMEM((N, 16, N), F32),
    "codes": pltpu.VMEM((N, 1, N), jnp.int32),
    "got_codes": pltpu.VMEM((N, 1, N), jnp.int32),
    "message": pltpu.VMEM((N, SENT, N), BF16),
    "got": pltpu.VMEM((N, SENT, N), BF16),
    "lhs": pltpu.VMEM((ROWS * C_OBS + ROWS, SLOTS), BF16),
    "rhs": pltpu.VMEM((SLOTS, 4 * N), BF16),
    "acc": pltpu.VMEM((ROWS * C_OBS + ROWS, 4 * N), F32),
    "wide_one": pltpu.VMEM((4 * N, N), F32),
    "wide_adj": pltpu.VMEM((256, 256), F32),
    "wide_two": pltpu.VMEM((CH, 9 * CH), F32),
    "left_one": pltpu.VMEM((256, 4 * N), BF16),
    "left_adj": pltpu.VMEM((512, 256), BF16),
    "left_two": pltpu.VMEM((N, 9 * CH), BF16),
    "wide_cot": pltpu.VMEM((CH, 8, N), F32),
    "cot": pltpu.VMEM((9, CH, N), F32),
    "cot_right": pltpu.VMEM((9, CH, N), F32),
    "cot_col": pltpu.VMEM((CH, N), F32),
    "cot_south": pltpu.VMEM((CH, N), F32),
    "cot_east": pltpu.VMEM((CH, N), F32),
    "cot_corner": pltpu.VMEM((CH, N), F32),
    "grad_act": pltpu.VMEM((8, 256, N), F32),
    "edge": pltpu.VMEM((2 * C_OBS, N), F32),
    "edge_west": pltpu.VMEM((2 * C_OBS, N), F32),
    "edge_corner": pltpu.VMEM((2 * C_OBS, N), F32),
    "north": pltpu.VMEM((C_OBS, 4 * N), F32),
    "north_thin": pltpu.VMEM((8, 4 * N), F32),
    "thin": pltpu.VMEM((ROWS + 1, 8, N), F32),
    "field_high": pltpu.VMEM((ROWS + 1, STEP_ONE, N), BF16),
    "field_low": pltpu.VMEM((ROWS + 1, STEP_ONE, N), BF16),
    "thin_high": pltpu.VMEM((ROWS // 2, 32, N), BF16),
    "thin_low": pltpu.VMEM((ROWS // 2, 32, N), BF16),
    "pre": pltpu.VMEM((ROWS // 2, N, N), F32),
    "act": pltpu.VMEM((ROWS // 2, N, N), F32),
    "act_edge": pltpu.VMEM((CH, N), F32),
    "act_west": pltpu.VMEM((CH, N), F32),
    "act_corner": pltpu.VMEM((CH, N), F32),
    "act_north": pltpu.VMEM((N, N), F32),
    "act_high": pltpu.VMEM((ROWS // 2 + 1, STEP_TWO, N), BF16),
    "act_low": pltpu.VMEM((ROWS // 2 + 1, STEP_TWO, N), BF16),
    "grad_one": pltpu.VMEM((9, C_OBS + 1, CH), F32),
    "grad_two": pltpu.VMEM((9, CH, CH), F32),
    "features": pltpu.VMEM((CH, 8, N), BF16),
    "wide_features": pltpu.VMEM((CH, 8, N), F32),
    "part": pltpu.VMEM((CH, 8 * N), F32),
    "total": pltpu.VMEM((CH, 8 * N), F32),
    "by_lon": pltpu.VMEM((16, 8, 4 * N), F32),
    "by_lat": pltpu.VMEM((8, 8, 4 * N), F32),
    "sent": pltpu.SemaphoreType.DMA((2,)),
    "came": pltpu.SemaphoreType.DMA((2, STEPS + 2)),
    "values": pltpu.VMEM((CAP, C_OBS, N), BF16),
    "blocks": pltpu.VMEM((CAP, N), jnp.int32),
    "counts": pltpu.VMEM((1, N), jnp.int32),
    "cot_in": pltpu.VMEM((CH, 8, N), BF16),
    "one": pltpu.VMEM((3, 3, C_OBS + 1, CH), F32),
    "two": pltpu.VMEM((3, 3, CH, CH), F32),
    "picker": pltpu.VMEM((N, 4 * N), BF16),
    "fetch": pltpu.SemaphoreType.DMA((7,)),
    "met": pltpu.SemaphoreType.REGULAR,
    "own": pltpu.SemaphoreType.DMA((2,)),
    "result": pltpu.SemaphoreType.DMA((3,)),
    "halo_sent": pltpu.SemaphoreType.DMA((10,)),
    "halo_came": pltpu.SemaphoreType.DMA((10,)),
    "sum_sent": pltpu.SemaphoreType.DMA((40,)),
    "sum_came": pltpu.SemaphoreType.DMA((40,)),
}


def whole_kernel(
    values_ref, w_ref, blocks_ref, counts_ref, one_ref, two_ref, cot_ref,
    features_ref, grad_one_ref, grad_two_ref, *scratch,
):
    m = Named(SCRATCH, scratch)
    lat, lon = position()
    me = lat * 16 + lon
    barrier = greet_near(lat, lon)
    fetched = [
        pltpu.make_async_copy(source, target, m.fetch.at[k])
        for k, (source, target) in enumerate((
            (values_ref, m.values), (blocks_ref, m.blocks), (counts_ref, m.counts),
            (w_ref, m.message.at[:, pl.ds(0, CAP)]),
            (cot_ref, m.cot_in), (one_ref, m.one), (two_ref, m.two),
        ))
    ]
    for copy in fetched:
        copy.start()
    arrange_picker(m.picker)

    north, south = lax.rem(lat + 7, 8), lax.rem(lat + 1, 8)
    west, east = lax.rem(lon + 15, 16), lax.rem(lon + 1, 16)

    def halo(k, source, target, device):
        return send_to(source, target, m.halo_sent.at[k], m.halo_came.at[k], device)

    pl.semaphore_wait(barrier, NEAR)
    for d in range(1, 16):
        pl.semaphore_signal(m.met, inc=1, device_id=(lat, lax.rem(lon + d, 16)), device_id_type=MESH)
    fetched[0].wait()
    m.wide[...] = m.values[...].astype(F32)
    pack_values(m.wide, m.turned, m.message)
    fetched[1].wait()
    fetched[2].wait()
    pack_codes(m.blocks, m.counts, m.codes)
    fetched[3].wait()
    streams = ((m.message, m.got), (m.codes, m.got_codes))
    mine = [
        pltpu.make_async_copy(source.at[me], target.at[0], m.own.at[k]) for k, (source, target) in enumerate(streams)
    ]
    for copy in mine:
        copy.start()
    def send(ordinal, carry):
        to_lat, to_lon = partner(lat, lon, ordinal)
        step = jnp.where(ordinal < STEPS * GROUP, ordinal // GROUP, ordinal // (GROUP // 2) - STEPS)
        to = to_lat * 16 + to_lon
        for k, (source, target) in enumerate(streams):
            send_to(
                source.at[to], target.at[ordinal], m.sent.at[k], m.came.at[k, step], (to_lat, to_lon)
            ).start()
        return carry

    fetched[4].wait()
    arrange_cotangent(m.cot_in, m.wide_cot, m.cot, m.cot_col)
    cot_halo = [
        halo(0, m.cot_col, m.cot_east, (lat, west)),
        halo(1, m.cot.at[0], m.cot_south, (north, lon)),
        halo(2, m.cot_col, m.cot_corner, (north, west)),
    ]
    cot_halo[0].start()
    cot_halo[1].start()
    pl.semaphore_wait(m.met, 15)
    cot_halo[2].start()
    lax.fori_loop(1, N, send, 0)

    fetched[5].wait()
    fetched[6].wait()
    arrange_kernels(m.one, m.two, m.wide_one, m.wide_adj, m.wide_two, m.left_one, m.left_adj, m.left_two)
    m.acc[...] = jnp.zeros_like(m.acc)
    for copy in cot_halo:
        copy.wait()
    back_to_activation(
        lat, m.cot, m.cot_south, m.cot_east, m.cot_corner, m.cot_right, m.left_adj, m.grad_act
    )
    for copy in mine:
        copy.wait()

    def arrive(first, count, step):
        for k, (_, target) in enumerate(streams):
            part = target.at[pl.ds(first, count)]
            pltpu.make_async_copy(part, part, m.came.at[k, step]).wait()

    def spread(first, group):
        spread_group(first, group, m.got, m.got_codes, m.picker, m.lhs, m.rhs, m.acc)

    def work(step, carry):
        @pl.when(step == 0)
        def _():
            arrive(1, GROUP - 1, 0)

        @pl.when(step > 0)
        def _():
            arrive(step * GROUP, GROUP, step)

        spread(step * GROUP, GROUP)
        return carry

    lax.fori_loop(0, STEPS, work, 0)

    def work_half(step, carry):
        first = STEPS * GROUP + step * (GROUP // 2)
        arrive(first, GROUP // 2, STEPS + step)
        spread(first, GROUP // 2)
        return carry

    lax.fori_loop(0, 2, work_half, 0)

    last = ROWS * C_OBS
    rows_halo = [
        halo(3, m.acc.at[pl.ds(last - C_OBS, C_OBS)], m.north, (south, lon)),
        halo(4, m.acc.at[pl.ds(last + ROWS - 8, 8)], m.north_thin, (south, lon)),
    ]
    edge_halo = [
        halo(5, m.edge, m.edge_west, (lat, east)),
        halo(6, m.edge, m.edge_corner, (south, east)),
    ]
    for copy in rows_halo:
        copy.start()
    field_edges(m.acc, m.edge)
    for copy in edge_halo:
        copy.start()
    split_inside(m.acc, m.thin, m.field_high, m.field_low)
    for copy in edge_halo + rows_halo:
        copy.wait()
    split_rim(
        lat, m.acc, m.north, m.north_thin, m.edge_west, m.edge_corner, m.thin,
        m.field_high, m.field_low, m.thin_high, m.thin_low,
    )
    field = (m.field_high, m.field_low, m.thin_high, m.thin_low)
    first_layer(*field, m.left_one, m.pre, m.act)
    act_halo = [
        halo(7, m.act.at[ROWS // 2 - 1], m.act_north, (south, lon)),
        halo(8, m.act_edge, m.act_west, (lat, east)),
        halo(9, m.act_edge, m.act_corner, (south, east)),
    ]
    act_halo[0].start()
    activation_edges(m.act, m.act_edge)
    act_halo[1].start()
    act_halo[2].start()
    grad_one = first_gradient(*field, m.pre, m.grad_act)
    pack_first_gradient(grad_one, m.part)
    split_activation_inside(m.act, m.act_high, m.act_low)
    for copy in act_halo:
        copy.wait()
    split_activation_rim(lat, m.act, m.act_north, m.act_west, m.act_corner, m.act_high, m.act_low)
    m.part[:, : 9 * CH] = second_gradient(m.act_high, m.act_low, m.cot)
    first_leg = sum_begin(lat, lon, m.part, m.by_lon, m.sum_sent, m.sum_came)
    second_layer(m.act_high, m.act_low, m.left_two, m.wide_features)
    m.features[...] = m.wide_features[...].astype(BF16)
    results = [
        pltpu.make_async_copy(m.features, features_ref, m.result.at[0]),
        pltpu.make_async_copy(m.grad_one, grad_one_ref, m.result.at[1]),
        pltpu.make_async_copy(m.grad_two, grad_two_ref, m.result.at[2]),
    ]
    results[0].start()
    sum_end(lat, lon, first_leg, m.part, m.total, m.by_lon, m.by_lat, m.sum_sent, m.sum_came)
    unpack_gradients(m.total, m.grad_one, m.grad_two)
    results[1].start()
    results[2].start()
    for k, (_, target) in enumerate(streams):
        everything = target.at[pl.ds(0, N - 1)]
        pltpu.make_async_copy(everything, everything, m.sent.at[k]).wait()
    for copy in results:
        copy.wait()


def hand_on_kernel(*refs):
    for k in range(3):
        refs[3 + k][...] = refs[k][...]


def on_device(
    obs_values, kernel_weights, pixel_blocks, obs_counts, kernel_one, kernel_two, cotangent
):
    vmem, anywhere = pl.BlockSpec(memory_space=pltpu.VMEM), pl.BlockSpec(memory_space=pl.ANY)
    outputs = (
        jax.ShapeDtypeStruct((CH, 8, N), BF16),
        jax.ShapeDtypeStruct((9, C_OBS + 1, CH), F32),
        jax.ShapeDtypeStruct((9, CH, CH), F32),
    )
    results = pl.pallas_call(
        whole_kernel,
        out_shape=outputs,
        in_specs=[anywhere] * 7,
        out_specs=(anywhere,) * 3,
        scratch_shapes=list(SCRATCH.values()),
        compiler_params=pltpu.CompilerParams(collective_id=0, has_side_effects=True, vmem_limit_bytes=56 << 20),
    )(
        obs_values[0].transpose(1, 2, 0),
        kernel_weights[0],
        pixel_blocks[0].T,
        obs_counts,
        kernel_one.transpose(0, 1, 3, 2),
        kernel_two,
        cotangent,
    )
    features, grad_one, grad_two = pl.pallas_call(
        hand_on_kernel,
        out_shape=outputs,
        in_specs=[vmem] * 3,
        out_specs=(vmem,) * 3,
        scratch_shapes=[pltpu.SemaphoreType.DMA((3,))],
    )(*results)
    grad_one = grad_one.reshape(3, 3, C_OBS + 1, CH).transpose(0, 1, 3, 2)
    return features, grad_one, grad_two.reshape(3, 3, CH, CH)


def solution(mesh):
    placed = (
        P(("lat", "lon"), None, None, None),
        P(("lat", "lon"), None, None, None),
        P(("lat", "lon"), None, None),
        P(("lat", "lon"), None),
        P(),
        P(),
        P(None, "lat", "lon"),
    )
    return jax.shard_map(
        on_device,
        mesh=mesh,
        in_specs=placed,
        out_specs=(P(None, "lat", "lon"), P(), P()),
        check_vma=False,
    )
```

```python
import jax
import jax.numpy as jnp
from jax import lax
from jax.experimental import pallas as pl
from jax.experimental.pallas import tpu as pltpu
from jax.sharding import PartitionSpec as P

MESH = pl.DeviceIdType.MESH
F32, BF16 = jnp.float32, jnp.bfloat16
N = 128
CAP = 64
GROUP = 16
STEPS = N // GROUP - 1
SLOTS = GROUP * CAP
SENT = CAP + 16
ROWS = 32
C_OBS = 32


def position():
    return lax.axis_index("lat"), lax.axis_index("lon")


def partner(lat, lon, ordinal):
    mixed = lax.rem(ordinal * 37, N)
    z = lax.rem(lat // 2 + lax.rem(mixed // 2, 4), 4)
    core = lax.rem(lat + lax.rem(mixed, 2), 2)
    x = lax.rem(lon // 4 + lax.rem(mixed // 8, 4), 4)
    y = lax.rem(lon + mixed // 32, 4)
    return z * 2 + core, x * 4 + y


NEAR = 22


def greet_near(lat, lon):
    barrier = pltpu.get_barrier_semaphore()
    for d in range(1, 16):
        pl.semaphore_signal(barrier, inc=1, device_id=(lat, lax.rem(lon + d, 16)), device_id_type=MESH)
    for d in range(1, 8):
        pl.semaphore_signal(barrier, inc=1, device_id=(lax.rem(lat + d, 8), lon), device_id_type=MESH)
    return barrier


def pack_values(wide_ref, turned_ref, message_ref):
    for i in range(16):
        pair = jnp.concatenate([wide_ref[:, i, :], wide_ref[:, 16 + i, :]], axis=0)
        turned_ref[:, i, :] = pair.T
    message_ref[:, CAP:, :] = turned_ref[...].astype(BF16)


def pack_codes(blocks_ref, counts_ref, codes_ref):
    slot = lax.broadcasted_iota(jnp.int32, (CAP, N), 0)
    code = jnp.where(slot < counts_ref[...], blocks_ref[...], 4 * ROWS)
    turned = jnp.concatenate([code, code], axis=0).astype(F32).T.astype(jnp.int32)
    codes_ref[:, 0, :] = turned


def spread_group(first, group, got, got_c, perm_ref, lhs_ref, rhs_ref, acc_ref):
    slots = group * CAP
    lane = lax.broadcasted_iota(jnp.int32, (1, N), 1)
    codes = got_c[pl.ds(first, group), 0, :]
    row_parts, value_parts = [], []
    for p in range(group // 2):
        even, odd = codes[2 * p : 2 * p + 1], codes[2 * p + 1 : 2 * p + 2]
        row_parts.append(jnp.where(lane < CAP, even, odd))
        one = got[first + 2 * p, CAP:, :].astype(F32)
        two = got[first + 2 * p + 1, CAP:, :].astype(F32)
        upper = jnp.where(lane < CAP, one, pltpu.roll(two, CAP, 1))
        lower = jnp.where(lane < CAP, pltpu.roll(one, CAP, 1), two)
        value_parts.append(jnp.concatenate([upper, lower], axis=0))
    row_of = jnp.broadcast_to(jnp.concatenate(row_parts, axis=1) // 4, (C_OBS, slots)).astype(F32).astype(BF16)
    values = jnp.concatenate(value_parts, axis=1).astype(BF16)
    zero = jnp.zeros_like(values)
    for r in range(ROWS):
        lhs_ref[r * C_OBS : (r + 1) * C_OBS, :slots] = jnp.where(row_of == jnp.array(r, BF16), values, zero)
    rows = lax.broadcasted_iota(jnp.int32, (ROWS, slots), 0).astype(F32).astype(BF16)
    lhs_ref[ROWS * C_OBS :, :slots] = jnp.where(row_of == rows, jnp.ones_like(values), zero)
    quarter = lax.rem(codes, 4).astype(F32).T
    lane_quarter = (lax.broadcasted_iota(jnp.int32, (CAP, N), 1) // 32).astype(F32)
    for s in range(group):
        keep = jnp.where(quarter[:CAP, s : s + 1] == lane_quarter, 1.0, 0.0).astype(BF16)
        pixels = jnp.dot(got[first + s, :CAP, :], perm_ref[...], preferred_element_type=F32).astype(BF16)
        for phase in range(4):
            rhs_ref[s * CAP : (s + 1) * CAP, phase * N : (phase + 1) * N] = (
                pixels[:, phase * N : (phase + 1) * N] * keep
            )
    acc_ref[...] += jnp.dot(lhs_ref[:, :slots], rhs_ref[:slots, :], preferred_element_type=F32)


def send_to(source, target, sent, came, device):
    return pltpu.make_async_remote_copy(
        src_ref=source, dst_ref=target, send_sem=sent, recv_sem=came, device_id=device, device_id_type=MESH
    )


AROUND = sorted(
    ((dx, dy) for dx in range(4) for dy in range(4) if dx + dy > 0),
    key=lambda at: -min(at[0], 4 - at[0]) - min(at[1], 4 - at[1]),
)


def around(lon, at):
    return lax.rem(lon // 4 + at[0], 4) * 4 + lax.rem(lon + at[1], 4)


def sixteenth(ref, p):
    rows = pl.ds(pl.multiple_of(8 * (p // 2), 8), 8)
    return ref.at[rows, pl.ds(pl.multiple_of(512 * lax.rem(p, 2), 512), 512)]


def sum_begin(lat, lon, part_ref, by_lon, sent, came):
    copies = []
    for d, at in enumerate(AROUND, 1):
        to = around(lon, at)
        copies.append(send_to(sixteenth(part_ref, to), by_lon.at[d], sent.at[d], came.at[d], (lat, to)))
    for copy in copies:
        copy.start()
    return copies


def sum_end(lat, lon, copies, part_ref, total_ref, by_lon, by_lat, sent, came):
    for copy in copies:
        copy.wait_recv()
    total = sixteenth(part_ref, lon)[...]
    for d in range(1, 16):
        total = total + by_lon[d]
    by_lat[lat] = total
    across = []
    for d, (dz, core) in enumerate(((2, 0), (2, 1), (1, 0), (3, 0), (1, 1), (3, 1), (0, 1)), 1):
        to = lax.rem(lat // 2 + dz, 4) * 2 + lax.rem(lat + core, 2)
        across.append(send_to(by_lat.at[lat], by_lat.at[lat], sent.at[16 + d], came.at[16 + d], (to, lon)))
    for copy in across:
        copy.start()
    for copy in across:
        copy.wait_recv()
    total = by_lat[0]
    for d in range(1, 8):
        total = total + by_lat[d]
    mine = sixteenth(total_ref, lon)
    mine[...] = total
    back = []
    for d, at in enumerate(AROUND, 1):
        back.append(send_to(mine, mine, sent.at[24 + d], came.at[24 + d], (lat, around(lon, at))))
    for copy in back:
        copy.start()
    for copy in back:
        copy.wait_recv()
    for copy in copies + across + back:
        copy.wait_send()


CH = 64
STEP_ONE = 5 * C_OBS
STEP_TWO = 3 * CH


def halves(value):
    high = value.astype(BF16)
    return high, (value - high.astype(F32)).astype(BF16)


def dot_nt(a, b):
    return lax.dot_general(a, b, (((1,), (1,)), ((), ())), preferred_element_type=F32)


def dot(a, b):
    return jnp.dot(a, b, preferred_element_type=F32)


def lanes(rows):
    return lax.broadcasted_iota(jnp.int32, (rows, N), 1)


def pack_column(total, place, column):
    return jnp.where(lanes(total.shape[0]) == place, jnp.broadcast_to(column, total.shape), total)


def enter_west(value, column):
    moved = pltpu.roll(value, 1, 1)
    return jnp.where(lanes(value.shape[0]) == 0, jnp.broadcast_to(column, value.shape), moved)


def enter_east(value, column):
    moved = pltpu.roll(value, N - 1, 1)
    return jnp.where(lanes(value.shape[0]) == N - 1, jnp.broadcast_to(column, value.shape), moved)


def arrange_kernels(one_ref, two_ref, wide_one, wide_adj, wide_two, left_one, left_adj, left_two):
    wide_one[...] = jnp.zeros_like(wide_one)
    wide_adj[...] = jnp.zeros_like(wide_adj)
    for a in range(3):
        for tap in range(5):
            row = a * STEP_ONE + tap * C_OBS
            thin = 3 * STEP_ONE + a * 8 + tap
            for half, e in ((0, tap), (1, tap - 2)):
                if 0 <= e < 3:
                    at = slice(half * CH, half * CH + CH)
                    wide_one[row : row + C_OBS, at] = one_ref[a, e, :C_OBS, :]
                    wide_one[thin : thin + 1, at] = one_ref[a, e, C_OBS:, :]
        for e in range(3):
            at = (a * 3 + e) * CH
            wide_two[:, at : at + CH] = two_ref[a, e]
    for lower in range(2):
        for east in range(2):
            for down in range(lower + 1):
                for right in range(east + 1):
                    a = 1 if lower == 0 else 2 - 2 * down
                    e = 1 if east == 0 else 2 - 2 * right
                    row, col = (down * 2 + right) * CH, (lower * 2 + east) * CH
                    wide_adj[row : row + CH, col : col + CH] = two_ref[a, e]
    for wide, left, turn in ((wide_one, left_one, True), (wide_adj, left_adj, True), (wide_two, left_two, False)):
        value = wide[...].T if turn else wide[...]
        high, low = halves(value)
        rows = value.shape[0]
        left[:rows, :] = high
        left[rows:, :] = low


def arrange_cotangent(cot_ref, wide_cot, cot, cot_col):
    wide_cot[...] = cot_ref[...].astype(F32)
    packed = jnp.zeros((CH, N), F32)
    for g in range(8):
        value = wide_cot[:, g, :]
        cot[g] = value
        packed = pack_column(packed, g, value[:, :1])
    cot_col[...] = packed


def back_to_activation(lat, cot, from_south, from_east, from_corner, right, left_adj, grad_act):
    cot[8] = jnp.where(lat < 7, from_south[...], 0.0)
    edge = from_east[...]
    for g in range(9):
        column = edge[:, g : g + 1] if g < 8 else jnp.where(lat < 7, from_corner[:, :1], 0.0)
        right[g] = enter_east(cot[g], column)

    def pair(p, carry):
        stack = [
            jnp.concatenate([cot[g], right[g], cot[g + 1], right[g + 1]], axis=0).astype(BF16)
            for g in (2 * p, 2 * p + 1)
        ]
        both = dot(left_adj[...], jnp.concatenate(stack, axis=1))
        both = both[:256] + both[256:]
        grad_act[2 * p] = both[:, :N]
        grad_act[2 * p + 1] = both[:, N:]
        return carry

    lax.fori_loop(0, 4, pair, 0)


def field_edges(acc_ref, edge_ref):
    packed = jnp.zeros((C_OBS, N), F32)
    for r in range(ROWS):
        packed = pack_column(packed, r, acc_ref[r * C_OBS : (r + 1) * C_OBS, 4 * N - 1 :])
    edge_ref[:C_OBS, :] = packed
    edge_ref[C_OBS:, :] = acc_ref[ROWS * C_OBS :, 3 * N :]


def split_inside(acc_ref, thin, high_ref, low_ref):
    for r in range(ROWS):
        for phase in range(4):
            high, low = halves(acc_ref[r * C_OBS : (r + 1) * C_OBS, phase * N : (phase + 1) * N])
            at = slice((phase + 1) * C_OBS, (phase + 2) * C_OBS)
            high_ref[r + 1, at, :] = high
            low_ref[r + 1, at, :] = low
    thin[...] = jnp.zeros_like(thin)
    for phase in range(4):
        thin[1 : ROWS + 1, phase + 1, :] = acc_ref[ROWS * C_OBS :, phase * N : (phase + 1) * N]


def split_rim(lat, acc_ref, north, north_thin, from_west, from_corner, thin, high_ref, low_ref, thin_high, thin_low):
    for r in range(ROWS):
        moved = enter_west(acc_ref[r * C_OBS : (r + 1) * C_OBS, 3 * N :], from_west[:C_OBS, r : r + 1])
        high, low = halves(moved)
        high_ref[r + 1, :C_OBS, :] = high
        low_ref[r + 1, :C_OBS, :] = low
    inside = lat > 0
    phases = [jnp.where(inside, north[:, phase * N : (phase + 1) * N], 0.0) for phase in range(4)]
    corner = jnp.where(inside, from_corner[:C_OBS, ROWS - 1 : ROWS], 0.0)
    high, low = halves(jnp.concatenate([enter_west(phases[3], corner)] + phases, axis=0))
    high_ref[0] = high
    low_ref[0] = low
    for phase in range(4):
        at = slice(phase * N, (phase + 1) * N)
        thin[0, phase + 1 : phase + 2, :] = jnp.where(inside, north_thin[7:8, at], 0.0)
    thin[1 : ROWS + 1, 0, :] = enter_west(acc_ref[ROWS * C_OBS :, 3 * N :], from_west[C_OBS:, N - 1 :])
    corner = enter_west(north_thin[7:8, 3 * N :], from_corner[2 * C_OBS - 1 :, N - 1 :])
    thin[0, 0:1, :] = jnp.where(inside, corner, 0.0)
    for h in range(ROWS // 2):
        rows = [thin[2 * h], thin[2 * h + 1], thin[2 * h + 2], jnp.zeros((8, N), F32)]
        high, low = halves(jnp.concatenate(rows, axis=0))
        thin_high[h] = high
        thin_low[h] = low


def taps_one(h, field, thin):
    return jnp.concatenate([field[2 * h], field[2 * h + 1], field[2 * h + 2], thin[h]], axis=0)


def taps_two(h, act):
    return jnp.concatenate([act[2 * h], act[2 * h + 1], act[2 * h + 2]], axis=0)


def beside(function, p, *refs):
    return jnp.concatenate([function(2 * p, *refs), function(2 * p + 1, *refs)], axis=1)


def first_layer(field_high, field_low, thin_high, thin_low, left_one, pre, act):
    def pair(p, carry):
        both = dot(left_one[...], beside(taps_one, p, field_high, thin_high))
        out = both[:N] + both[N:] + dot(left_one[:N, :], beside(taps_one, p, field_low, thin_low))
        active = out / (1.0 + jnp.exp(-out))
        for k in range(2):
            pre[2 * p + k] = out[:, k * N : (k + 1) * N]
            act[2 * p + k] = active[:, k * N : (k + 1) * N]
        return carry

    lax.fori_loop(0, ROWS // 4, pair, 0, unroll=8)


def first_gradient(field_high, field_low, thin_high, thin_low, pre, grad_act):
    def row(h, g, lower):
        value = pre[h]
        s = 1.0 / (1.0 + jnp.exp(-value))
        return grad_act[g, lower * N : (lower + 1) * N, :] * (s * (1.0 + value * (1.0 - s)))

    def pair(p, total):
        grad = jnp.concatenate([row(2 * p, p, 0), row(2 * p + 1, p, 1)], axis=1)
        high, low = halves(grad)
        field = beside(taps_one, p, field_high, thin_high)
        both = dot_nt(jnp.concatenate([high, low], axis=0), field)
        return total + (both[:N] + both[N:]) + dot_nt(high, beside(taps_one, p, field_low, thin_low))

    return lax.fori_loop(0, ROWS // 4, pair, jnp.zeros((N, 4 * N), F32), unroll=8)


def activation_edges(act, edge_ref):
    packed = jnp.zeros((CH, N), F32)
    for y in range(ROWS // 2):
        packed = pack_column(packed, y, act[y, CH:, N - 1 :])
    edge_ref[...] = packed


def split_activation_inside(act, high_ref, low_ref):
    for y in range(ROWS // 2):
        high, low = halves(act[y])
        high_ref[y + 1, CH:, :] = high
        low_ref[y + 1, CH:, :] = low


def split_activation_rim(lat, act, north, from_west, from_corner, high_ref, low_ref):
    for y in range(ROWS // 2):
        high, low = halves(enter_west(act[y, CH:, :], from_west[:, y : y + 1]))
        high_ref[y + 1, :CH, :] = high
        low_ref[y + 1, :CH, :] = low
    last = ROWS // 2 - 1
    value = jnp.where(lat > 0, north[...], 0.0)
    column = jnp.where(lat > 0, from_corner[:, last : last + 1], 0.0)
    high, low = halves(jnp.concatenate([enter_west(value[CH:], column), value], axis=0))
    high_ref[0] = high
    low_ref[0] = low


def second_gradient(act_high, act_low, cot):
    total = jnp.zeros((CH, 9 * CH), F32)
    for p in range(4):
        grad = jnp.concatenate([cot[2 * p], cot[2 * p + 1]], axis=1).astype(BF16)
        total = total + (dot_nt(grad, beside(taps_two, p, act_high)) + dot_nt(grad, beside(taps_two, p, act_low)))
    return total


def second_layer(act_high, act_low, left_two, wide_features):
    for p in range(4):
        both = dot(left_two[...], beside(taps_two, p, act_high))
        out = both[:CH] + both[CH:] + dot(left_two[:CH, :], beside(taps_two, p, act_low))
        for k in range(2):
            wide_features[:, 2 * p + k, :] = out[:, k * N : (k + 1) * N]


def pack_first_gradient(one, part_ref):
    lane = lax.broadcasted_iota(jnp.int32, (CH, 4 * N), 1)
    upper, lower = one[:CH], one[CH:]
    moved = jnp.where(lane < 3 * STEP_ONE, pltpu.roll(lower, 4 * N - 2 * C_OBS, 1), pltpu.roll(lower, 4 * N - 2, 1))
    both = upper + moved
    tight = jnp.where(
        lane < 96, both,
        jnp.where(
            lane < 192, pltpu.roll(both, 4 * N - 64, 1),
            jnp.where(lane < 288, pltpu.roll(both, 4 * N - 128, 1), pltpu.roll(both, 4 * N - 192, 1)),
        ),
    )
    shifted = pltpu.roll(tight, CH, 1)
    part_ref[:, 4 * N :] = shifted


def unpack_gradients(total_ref, one_ref, two_ref):
    for i in range(9):
        two_ref[i] = total_ref[:, i * CH : (i + 1) * CH]
    turned = total_ref[:, 4 * N : 7 * N].T
    for i in range(9):
        one_ref[i, :C_OBS, :] = turned[CH + i * C_OBS : CH + (i + 1) * C_OBS]
        thin = CH + 9 * C_OBS + (i // 3) * 8 + i % 3
        one_ref[i, C_OBS:, :] = turned[thin : thin + 1]


def arrange_picker(picker_ref):
    lane = lax.broadcasted_iota(jnp.int32, (N, 4 * N), 1)
    pixel = lax.broadcasted_iota(jnp.int32, (N, 4 * N), 0)
    picker_ref[...] = jnp.where(pixel == 4 * lax.rem(lane, 32) + lane // N, 1.0, 0.0).astype(BF16)


class Named:
    def __init__(self, names, refs):
        self.__dict__.update(zip(names, refs))


SCRATCH = {
    "wide": pltpu.VMEM((CAP, C_OBS, N), F32),
    "turned": pltpu.VMEM((N, 16, N), F32),
    "codes": pltpu.VMEM((N, 1, N), jnp.int32),
    "got_codes": pltpu.VMEM((N, 1, N), jnp.int32),
    "message": pltpu.VMEM((N, SENT, N), BF16),
    "got": pltpu.VMEM((N, SENT, N), BF16),
    "lhs": pltpu.VMEM((ROWS * C_OBS + ROWS, SLOTS), BF16),
    "rhs": pltpu.VMEM((SLOTS, 4 * N), BF16),
    "acc": pltpu.VMEM((ROWS * C_OBS + ROWS, 4 * N), F32),
    "wide_one": pltpu.VMEM((4 * N, N), F32),
    "wide_adj": pltpu.VMEM((256, 256), F32),
    "wide_two": pltpu.VMEM((CH, 9 * CH), F32),
    "left_one": pltpu.VMEM((256, 4 * N), BF16),
    "left_adj": pltpu.VMEM((512, 256), BF16),
    "left_two": pltpu.VMEM((N, 9 * CH), BF16),
    "wide_cot": pltpu.VMEM((CH, 8, N), F32),
    "cot": pltpu.VMEM((9, CH, N), F32),
    "cot_right": pltpu.VMEM((9, CH, N), F32),
    "cot_col": pltpu.VMEM((CH, N), F32),
    "cot_south": pltpu.VMEM((CH, N), F32),
    "cot_east": pltpu.VMEM((CH, N), F32),
    "cot_corner": pltpu.VMEM((CH, N), F32),
    "grad_act": pltpu.VMEM((8, 256, N), F32),
    "edge": pltpu.VMEM((2 * C_OBS, N), F32),
    "edge_west": pltpu.VMEM((2 * C_OBS, N), F32),
    "edge_corner": pltpu.VMEM((2 * C_OBS, N), F32),
    "north": pltpu.VMEM((C_OBS, 4 * N), F32),
    "north_thin": pltpu.VMEM((8, 4 * N), F32),
    "thin": pltpu.VMEM((ROWS + 1, 8, N), F32),
    "field_high": pltpu.VMEM((ROWS + 1, STEP_ONE, N), BF16),
    "field_low": pltpu.VMEM((ROWS + 1, STEP_ONE, N), BF16),
    "thin_high": pltpu.VMEM((ROWS // 2, 32, N), BF16),
    "thin_low": pltpu.VMEM((ROWS // 2, 32, N), BF16),
    "pre": pltpu.VMEM((ROWS // 2, N, N), F32),
    "act": pltpu.VMEM((ROWS // 2, N, N), F32),
    "act_edge": pltpu.VMEM((CH, N), F32),
    "act_west": pltpu.VMEM((CH, N), F32),
    "act_corner": pltpu.VMEM((CH, N), F32),
    "act_north": pltpu.VMEM((N, N), F32),
    "act_high": pltpu.VMEM((ROWS // 2 + 1, STEP_TWO, N), BF16),
    "act_low": pltpu.VMEM((ROWS // 2 + 1, STEP_TWO, N), BF16),
    "grad_one": pltpu.VMEM((9, C_OBS + 1, CH), F32),
    "grad_two": pltpu.VMEM((9, CH, CH), F32),
    "features": pltpu.VMEM((CH, 8, N), BF16),
    "wide_features": pltpu.VMEM((CH, 8, N), F32),
    "part": pltpu.VMEM((CH, 8 * N), F32),
    "total": pltpu.VMEM((CH, 8 * N), F32),
    "by_lon": pltpu.VMEM((16, 8, 4 * N), F32),
    "by_lat": pltpu.VMEM((8, 8, 4 * N), F32),
    "sent": pltpu.SemaphoreType.DMA((2,)),
    "came": pltpu.SemaphoreType.DMA((2, STEPS + 2)),
    "values": pltpu.VMEM((CAP, C_OBS, N), BF16),
    "blocks": pltpu.VMEM((CAP, N), jnp.int32),
    "counts": pltpu.VMEM((1, N), jnp.int32),
    "cot_in": pltpu.VMEM((CH, 8, N), BF16),
    "one": pltpu.VMEM((3, 3, C_OBS + 1, CH), F32),
    "two": pltpu.VMEM((3, 3, CH, CH), F32),
    "picker": pltpu.VMEM((N, 4 * N), BF16),
    "fetch": pltpu.SemaphoreType.DMA((7,)),
    "met": pltpu.SemaphoreType.REGULAR,
    "own": pltpu.SemaphoreType.DMA((2,)),
    "result": pltpu.SemaphoreType.DMA((3,)),
    "halo_sent": pltpu.SemaphoreType.DMA((10,)),
    "halo_came": pltpu.SemaphoreType.DMA((10,)),
    "sum_sent": pltpu.SemaphoreType.DMA((40,)),
    "sum_came": pltpu.SemaphoreType.DMA((40,)),
}


def whole_kernel(
    values_ref, w_ref, blocks_ref, counts_ref, one_ref, two_ref, cot_ref,
    features_ref, grad_one_ref, grad_two_ref, *scratch,
):
    m = Named(SCRATCH, scratch)
    lat, lon = position()
    me = lat * 16 + lon
    barrier = greet_near(lat, lon)
    fetched = [
        pltpu.make_async_copy(source, target, m.fetch.at[k])
        for k, (source, target) in enumerate((
            (values_ref, m.values), (blocks_ref, m.blocks), (counts_ref, m.counts),
            (w_ref, m.message.at[:, pl.ds(0, CAP)]),
            (cot_ref, m.cot_in), (one_ref, m.one), (two_ref, m.two),
        ))
    ]
    for copy in fetched:
        copy.start()
    arrange_picker(m.picker)

    north, south = lax.rem(lat + 7, 8), lax.rem(lat + 1, 8)
    west, east = lax.rem(lon + 15, 16), lax.rem(lon + 1, 16)

    def halo(k, source, target, device):
        return send_to(source, target, m.halo_sent.at[k], m.halo_came.at[k], device)

    pl.semaphore_wait(barrier, NEAR)
    for d in range(1, 16):
        pl.semaphore_signal(m.met, inc=1, device_id=(lat, lax.rem(lon + d, 16)), device_id_type=MESH)
    fetched[0].wait()
    m.wide[...] = m.values[...].astype(F32)
    pack_values(m.wide, m.turned, m.message)
    fetched[1].wait()
    fetched[2].wait()
    pack_codes(m.blocks, m.counts, m.codes)
    fetched[3].wait()
    streams = ((m.message, m.got), (m.codes, m.got_codes))
    mine = [
        pltpu.make_async_copy(source.at[me], target.at[0], m.own.at[k]) for k, (source, target) in enumerate(streams)
    ]
    for copy in mine:
        copy.start()
    def send(ordinal, carry):
        to_lat, to_lon = partner(lat, lon, ordinal)
        step = jnp.where(ordinal < STEPS * GROUP, ordinal // GROUP, ordinal // (GROUP // 2) - STEPS)
        to = to_lat * 16 + to_lon
        for k, (source, target) in enumerate(streams):
            send_to(
                source.at[to], target.at[ordinal], m.sent.at[k], m.came.at[k, step], (to_lat, to_lon)
            ).start()
        return carry

    fetched[4].wait()
    arrange_cotangent(m.cot_in, m.wide_cot, m.cot, m.cot_col)
    cot_halo = [
        halo(0, m.cot_col, m.cot_east, (lat, west)),
        halo(1, m.cot.at[0], m.cot_south, (north, lon)),
        halo(2, m.cot_col, m.cot_corner, (north, west)),
    ]
    cot_halo[0].start()
    cot_halo[1].start()
    pl.semaphore_wait(m.met, 15)
    cot_halo[2].start()
    lax.fori_loop(1, N, send, 0)

    fetched[5].wait()
    fetched[6].wait()
    arrange_kernels(m.one, m.two, m.wide_one, m.wide_adj, m.wide_two, m.left_one, m.left_adj, m.left_two)
    m.acc[...] = jnp.zeros_like(m.acc)
    for copy in cot_halo:
        copy.wait()
    back_to_activation(
        lat, m.cot, m.cot_south, m.cot_east, m.cot_corner, m.cot_right, m.left_adj, m.grad_act
    )
    for copy in mine:
        copy.wait()

    def arrive(first, count, step):
        for k, (_, target) in enumerate(streams):
            part = target.at[pl.ds(first, count)]
            pltpu.make_async_copy(part, part, m.came.at[k, step]).wait()

    def spread(first, group):
        spread_group(first, group, m.got, m.got_codes, m.picker, m.lhs, m.rhs, m.acc)

    def work(step, carry):
        @pl.when(step == 0)
        def _():
            arrive(1, GROUP - 1, 0)

        @pl.when(step > 0)
        def _():
            arrive(step * GROUP, GROUP, step)

        spread(step * GROUP, GROUP)
        return carry

    lax.fori_loop(0, STEPS, work, 0)

    def work_half(step, carry):
        first = STEPS * GROUP + step * (GROUP // 2)
        arrive(first, GROUP // 2, STEPS + step)
        spread(first, GROUP // 2)
        return carry

    lax.fori_loop(0, 2, work_half, 0)

    last = ROWS * C_OBS
    rows_halo = [
        halo(3, m.acc.at[pl.ds(last - C_OBS, C_OBS)], m.north, (south, lon)),
        halo(4, m.acc.at[pl.ds(last + ROWS - 8, 8)], m.north_thin, (south, lon)),
    ]
    edge_halo = [
        halo(5, m.edge, m.edge_west, (lat, east)),
        halo(6, m.edge, m.edge_corner, (south, east)),
    ]
    for copy in rows_halo:
        copy.start()
    field_edges(m.acc, m.edge)
    for copy in edge_halo:
        copy.start()
    split_inside(m.acc, m.thin, m.field_high, m.field_low)
    for copy in edge_halo + rows_halo:
        copy.wait()
    split_rim(
        lat, m.acc, m.north, m.north_thin, m.edge_west, m.edge_corner, m.thin,
        m.field_high, m.field_low, m.thin_high, m.thin_low,
    )
    field = (m.field_high, m.field_low, m.thin_high, m.thin_low)
    first_layer(*field, m.left_one, m.pre, m.act)
    act_halo = [
        halo(7, m.act.at[ROWS // 2 - 1], m.act_north, (south, lon)),
        halo(8, m.act_edge, m.act_west, (lat, east)),
        halo(9, m.act_edge, m.act_corner, (south, east)),
    ]
    act_halo[0].start()
    activation_edges(m.act, m.act_edge)
    act_halo[1].start()
    act_halo[2].start()
    grad_one = first_gradient(*field, m.pre, m.grad_act)
    pack_first_gradient(grad_one, m.part)
    split_activation_inside(m.act, m.act_high, m.act_low)
    for copy in act_halo:
        copy.wait()
    split_activation_rim(lat, m.act, m.act_north, m.act_west, m.act_corner, m.act_high, m.act_low)
    m.part[:, : 9 * CH] = second_gradient(m.act_high, m.act_low, m.cot)
    first_leg = sum_begin(lat, lon, m.part, m.by_lon, m.sum_sent, m.sum_came)
    second_layer(m.act_high, m.act_low, m.left_two, m.wide_features)
    m.features[...] = m.wide_features[...].astype(BF16)
    results = [
        pltpu.make_async_copy(m.features, features_ref, m.result.at[0]),
        pltpu.make_async_copy(m.grad_one, grad_one_ref, m.result.at[1]),
        pltpu.make_async_copy(m.grad_two, grad_two_ref, m.result.at[2]),
    ]
    results[0].start()
    sum_end(lat, lon, first_leg, m.part, m.total, m.by_lon, m.by_lat, m.sum_sent, m.sum_came)
    unpack_gradients(m.total, m.grad_one, m.grad_two)
    results[1].start()
    results[2].start()
    for k, (_, target) in enumerate(streams):
        everything = target.at[pl.ds(0, N - 1)]
        pltpu.make_async_copy(everything, everything, m.sent.at[k]).wait()
    for copy in results:
        copy.wait()


def hand_on_kernel(*refs):
    for k in range(3):
        refs[3 + k][...] = refs[k][...]


def on_device(
    obs_values, kernel_weights, pixel_blocks, obs_counts, kernel_one, kernel_two, cotangent
):
    vmem, anywhere = pl.BlockSpec(memory_space=pltpu.VMEM), pl.BlockSpec(memory_space=pl.ANY)
    outputs = (
        jax.ShapeDtypeStruct((CH, 8, N), BF16),
        jax.ShapeDtypeStruct((9, C_OBS + 1, CH), F32),
        jax.ShapeDtypeStruct((9, CH, CH), F32),
    )
    results = pl.pallas_call(
        whole_kernel,
        out_shape=outputs,
        in_specs=[anywhere] * 7,
        out_specs=(anywhere,) * 3,
        scratch_shapes=list(SCRATCH.values()),
        compiler_params=pltpu.CompilerParams(collective_id=0, has_side_effects=True, vmem_limit_bytes=56 << 20),
    )(
        obs_values[0].transpose(1, 2, 0),
        kernel_weights[0],
        pixel_blocks[0].T,
        obs_counts,
        kernel_one.transpose(0, 1, 3, 2),
        kernel_two,
        cotangent,
    )
    features, grad_one, grad_two = pl.pallas_call(
        hand_on_kernel,
        out_shape=outputs,
        in_specs=[vmem] * 3,
        out_specs=(vmem,) * 3,
        scratch_shapes=[pltpu.SemaphoreType.DMA((3,))],
    )(*results)
    grad_one = grad_one.reshape(3, 3, C_OBS + 1, CH).transpose(0, 1, 3, 2)
    return features, grad_one, grad_two.reshape(3, 3, CH, CH)


def solution(mesh):
    placed = (
        P(("lat", "lon"), None, None, None),
        P(("lat", "lon"), None, None, None),
        P(("lat", "lon"), None, None),
        P(("lat", "lon"), None),
        P(),
        P(),
        P(None, "lat", "lon"),
    )
    return jax.shard_map(
        on_device,
        mesh=mesh,
        in_specs=placed,
        out_specs=(P(None, "lat", "lon"), P(), P()),
        check_vma=False,
    )
```
